32 devices in a mesh: ka: 2 (over y), pb: 4 (over z), row: 4 (over x, core).
Axes of the slice: x: 2, y: 2, z: 4, core: 2. Of those that a mesh axis runs over, the one named last changes fastest.
Arguments:
- coupling: bfloat16 [16, 64, 20736], P('pb', ('ka', 'row')), may hold values from -1 to 1
- rotation: bfloat16 [16, 36, 36], P('pb'), may hold values from -1 to 1
- freq: float32 [16, 36], P('pb'), may hold values from 0.02 to 0.3
- eigvec: bfloat16 [256, 24, 24], P(('ka', 'row')), may hold values from -1.25 to 1.25
- energies: float32 [256, 24], P(('ka', 'row')), may hold values from -1.5 to 1.5
- window: int32 [256], P(('ka', 'row')), may hold values from 12 to 24
- kq_index: int32 [16, 256], P('pb'), may hold values from 0 to 255, as said below
- kpoints: float32 [256, 3], replicated, may hold values from 0 to 1
- lattice: int32 [64, 3], replicated, may hold values from -3 to 3
Outputs:
- electron: float32 [256, 24], P(('ka', 'row'))
- phonon: float32 [16, 36], P('pb')
The draws below stay inside these ranges and needn't reach their ends.
Inputs may be any that keep to these rules, and one draw needn't show every extreme that they name: The k-points form a shifted grid of 256 points, (256 // 64) x 8 x 8, listed in an order drawn from the seed; each q-point is a vector of that grid without the shift. kq_index[q, k] is the index of the k-point equal to kpoints[k] plus the q-point's vector modulo 1, so each row of kq_index is a permutation of 0 to 255.
All inputs are finite; a program needn't handle non-finite values.
Results may differ from the reference program's by a relative error of at most 0.00089.
Values may be sent and summed in bfloat16 or wider, within the bound.
No kernel may reach another device: no remote copies, remote signals or barrier semaphores. Data moves between devices by JAX's collectives and lax.ppermute only.
A program may use at most 128 MiB of HBM per device.

```python
import math
import jax
import jax.numpy as jnp
from jax import lax

NB = 24
NM = 36
NRE = 64
NK = 256
NQ = 16


def grid_parts(grid_index):
    first = grid_index // 64
    second = grid_index // 8 % 8
    third = grid_index % 8
    return (first, second, third)


def grid_common(key):
    order = jax.random.permutation(jax.random.fold_in(key, 311), NK).astype(jnp.int32)
    q_grid = jax.random.randint(jax.random.fold_in(key, 312), (NQ,), 0, NK).astype(jnp.int32)
    start_displacement = jax.random.uniform(jax.random.fold_in(key, 313), (3,), jnp.float32)
    return (order, q_grid, start_displacement)


def draw_kpoints(key, part):
    order, q_grid, start_displacement = grid_common(key)
    first_length = NK // 64
    first, second, third = grid_parts(order)
    coords = jnp.stack([(first.astype(jnp.float32) + start_displacement[0]) / first_length, (second.astype(jnp.float32) + start_displacement[1]) / 8.0, (third.astype(jnp.float32) + start_displacement[2]) / 8.0], axis=1)
    return jnp.clip(coords, 0.0, 0.999999).astype(jnp.float32)


def draw_kq_index(key, part):
    order, q_grid, start_displacement = grid_common(key)
    first_length = NK // 64
    inverse = jnp.argsort(order).astype(jnp.int32)
    k_first, k_second, k_third = grid_parts(order)
    q_first, q_second, q_third = grid_parts(q_grid)
    s_first = (k_first[None, :] + q_first[:, None]) % first_length
    middle_offset_index = (k_second[None, :] + q_second[:, None]) % 8
    s_third = (k_third[None, :] + q_third[:, None]) % 8
    target = (s_first * 64 + middle_offset_index * 8 + s_third).astype(jnp.int32)
    return jnp.take(inverse, target, axis=0).astype(jnp.int32)


def place_ends(entries, rng, least, top_value):
    longest = entries.shape.index(max(entries.shape))
    spots = []
    for shift in (0, 1):
        where = [jax.random.randint(jax.random.fold_in(rng, axis), (), 0, length) for axis, length in enumerate(entries.shape)]
        where[longest] = (where[longest] + shift) % entries.shape[longest]
        spots.append(tuple(where))
    return entries.at[spots[0]].set(least).at[spots[1]].set(top_value)


def block_scale(rng, extent, split, least, high):
    gain, own = 1.0, jax.random.fold_in(rng, 6)
    for axis_at, shards_of in split:
        steps = jnp.exp(jax.random.uniform(jax.random.fold_in(own, axis_at), (shards_of,), jnp.float32, least / len(split), high / len(split)))
        gain = gain * jnp.repeat(steps, extent[axis_at] // shards_of).reshape([-1 if axis == axis_at else 1 for axis in range(len(extent))])
    return gain


def normal_values(key, shape, width, bound, cuts=(), held_as=jnp.bfloat16):
    values = width * jax.random.normal(key, shape, jnp.float32)
    if cuts:
        values = values * block_scale(key, shape, cuts, -0.22, 0.18)
    return jnp.clip(values, -bound, bound).astype(held_as)


def setup_inputs(seed: int = 0) -> dict:
    key_list = jax.random.split(jax.random.key(seed), 10)
    coupling = normal_values(key_list[0], (NQ, NRE, NM * NB * NB), (NRE // 2) ** -0.5, 1.0, ((0, 4), (1, 8)))
    rotation = normal_values(key_list[1], (NQ, NM, NM), NM ** -0.5, 1.0, ((0, 4),))
    freq = jnp.clip(jnp.exp(math.log(0.3) - 2.7080503 * jax.random.uniform(key_list[2], (NQ, NM), jnp.float32) ** block_scale(key_list[2], (NQ, NM), ((0, 4),), -0.2, 0.2)), 0.02, 0.3)
    eigvec = normal_values(key_list[3], (NK, NB, NB), NB ** -0.5, 1.25, ((0, 8),))
    energies = jnp.clip(jax.random.uniform(key_list[4], (NK, NB), jnp.float32, -1.5, 1.5) * block_scale(key_list[4], (NK, NB), ((0, 8),), -0.4, 0.0), -1.5, 1.5)
    window = place_ends(jax.random.randint(key_list[5], (NK,), NB // 2, NB + 1), jax.random.fold_in(key_list[5], 1), NB // 2, NB).astype(jnp.int32)
    kq_index = draw_kq_index(jax.random.fold_in(key_list[9], 71), 0)
    kpoints = draw_kpoints(jax.random.fold_in(key_list[9], 71), 0)
    lattice = place_ends(jax.random.randint(key_list[8], (NRE, 3), -3, 4), jax.random.fold_in(key_list[8], 1), -3, 3).astype(jnp.int32)
    return {"coupling": coupling, "rotation": rotation, "freq": freq, "eigvec": eigvec, "energies": energies, "window": window, "kq_index": kq_index, "kpoints": kpoints, "lattice": lattice}


SIGMA = 0.1
THERMAL_ENERGY_KT = 0.2

def phase_table(lattice, kpoint_rows):
    rvec = lattice.astype(jnp.float32)
    argument = rvec[:, 0:1] * kpoint_rows[:, 0][None, :] + rvec[:, 1:2] * kpoint_rows[:, 1][None, :] + rvec[:, 2:3] * kpoint_rows[:, 2][None, :]
    return jnp.cos(2.0 * math.pi * argument).astype(jnp.bfloat16)

def reference(coupling, rotation, freq, eigvec, energies, window, kq_index, kpoints, lattice):
    block = min(NK, 128)
    count = NK // block
    limits = window.astype(jnp.float32)
    norm = 1.0 / (math.sqrt(2.0 * math.pi) * SIGMA)
    bands = jnp.arange(NB).astype(jnp.float32)

    def per_q(items):
        coup_q, rot_q, freq_q, kq_row = items

        def per_block(number):
            start = (number * block).astype(jnp.int32)
            kp_rows = lax.dynamic_slice(kpoints, (start, jnp.int32(0)), (block, 3))
            phase = phase_table(lattice, kp_rows)
            index = lax.dynamic_slice(kq_row, (start,), (block,))
            eig_k = lax.dynamic_slice(eigvec, (start, jnp.int32(0), jnp.int32(0)), (block, NB, NB))
            eig_kq = jnp.take(eigvec, index, axis=0)
            energy_initial_state = lax.dynamic_slice(energies, (start, jnp.int32(0)), (block, NB))
            energy_final_state = jnp.take(energies, index, axis=0)
            lim_k = lax.dynamic_slice(limits, (start,), (block,))
            lim_kq = jnp.take(limits, index, axis=0)
            bloch = jnp.dot(phase.T, coup_q, preferred_element_type=jnp.float32).astype(jnp.bfloat16)
            bloch = bloch.reshape(block, NM, NB, NB)
            modal = jnp.einsum('kamn,ab->kbmn', bloch.astype(jnp.float32), rot_q.astype(jnp.float32)).astype(jnp.bfloat16)
            right = jnp.einsum('kbmj,kjn->kbmn', modal.astype(jnp.float32), eig_k.astype(jnp.float32)).astype(jnp.bfloat16)
            coupled = jnp.einsum('kim,kbin->kbmn', eig_kq.astype(jnp.float32), right.astype(jnp.float32))
            diff = energy_final_state[:, None, :, None] - energy_initial_state[:, None, None, :] - freq_q[None, :, None, None]
            delta = jnp.exp(-(diff * diff) / (2.0 * SIGMA * SIGMA)) * norm
            mask_m = (bands[None, :] < lim_kq[:, None]).astype(jnp.float32)
            mask_n = (bands[None, :] < lim_k[:, None]).astype(jnp.float32)
            strength = coupled * coupled * delta * mask_m[:, None, :, None] * mask_n[:, None, None, :]
            fermi_filling_initial = jax.nn.sigmoid(-energy_initial_state / THERMAL_ENERGY_KT)
            fermi_filling_final = jax.nn.sigmoid(-energy_final_state / THERMAL_ENERGY_KT)
            elec = lax.optimization_barrier(jnp.sum(strength, axis=(1, 2)))
            phon = lax.optimization_barrier(jnp.sum(strength * (fermi_filling_initial[:, None, None, :] - fermi_filling_final[:, None, :, None]), axis=(0, 2, 3)))
            return (elec, phon)
        elec_blocks, vibration_mode_tiles = lax.map(per_block, jnp.arange(count))
        return (elec_blocks.reshape(NK, NB), lax.optimization_barrier(jnp.sum(vibration_mode_tiles, axis=0)))
    elec_q, phon_q = lax.map(per_q, (coupling, rotation, freq, kq_index))
    electron = lax.optimization_barrier(jnp.sum(elec_q, axis=0)) * (1.0 / (NQ * NM * NB))
    phonon = phon_q * (1.0 / (NK * NB))
    return (electron, phonon)
```

```python
import functools
import math

import jax
import jax.numpy as jnp
from jax import lax
from jax.experimental import pallas as pl
from jax.experimental.pallas import tpu as pltpu
from jax.sharding import PartitionSpec as P

SIGMA = 0.1
THERMAL_ENERGY_KT = 0.2
VMEM = pltpu.CompilerParams(vmem_limit_bytes=56 * 1024 * 1024)
F32 = jnp.float32
BF16 = jnp.bfloat16


def phase_table(lattice, kpoint_rows):
    rvec = lattice.astype(jnp.float32)
    argument = (
        rvec[:, 0:1] * kpoint_rows[:, 0][None, :]
        + rvec[:, 1:2] * kpoint_rows[:, 1][None, :]
        + rvec[:, 2:3] * kpoint_rows[:, 2][None, :]
    )
    return jnp.cos(2.0 * math.pi * argument).astype(jnp.bfloat16)


def iota(shape, dim):
    return lax.broadcasted_iota(jnp.int32, shape, dim)


def rotate_kernel(n_modes, n_bands, v_parts, coup_ref, rot_ref, out_ref):
    r = coup_ref.shape[1]
    pair = n_bands * n_bands
    rows = n_modes * r
    x = coup_ref[0].astype(F32)
    x = jnp.concatenate([x[:, c * pair : (c + 1) * pair] for c in range(n_modes)], axis=0).astype(BF16)
    rot = rot_ref[0]
    spread_v = (iota((rows, n_modes), 0) // r == iota((rows, n_modes), 1)).astype(BF16)
    spread_c = (iota((n_modes, rows), 1) // r == iota((n_modes, rows), 0)).astype(BF16)
    half = lax.dot_general(spread_v, rot, (((1,), (1,)), ((), ())), preferred_element_type=F32)
    full = jnp.dot(half.astype(BF16), spread_c, preferred_element_type=F32)
    same = iota((rows, rows), 0) % r == iota((rows, rows), 1) % r
    big = jnp.where(same, full, 0.0).astype(BF16)
    y = jnp.dot(big, x, preferred_element_type=F32)
    v_count = n_modes // v_parts
    for part in range(v_parts):
        for i in range(0, n_bands, 2):
            both = []
            for ii in (i, i + 1):
                both.append(
                    jnp.concatenate(
                        [
                            y[v * r : (v + 1) * r, ii * n_bands : (ii + 1) * n_bands]
                            for v in range(part * v_count, (part + 1) * v_count)
                        ],
                        axis=1,
                    )
                )
            out_ref[part, 0, i * r : (i + 2) * r, :] = jnp.concatenate(both, axis=0).astype(BF16)


def rotate(coupling, rotation, n_bands, v_parts):
    q, r, width = coupling.shape
    n_modes = rotation.shape[1]
    cols = n_modes // v_parts * n_bands
    return pl.pallas_call(
        functools.partial(rotate_kernel, n_modes, n_bands, v_parts),
        grid=(q,),
        in_specs=[
            pl.BlockSpec((1, r, width), lambda a: (a, 0, 0)),
            pl.BlockSpec((1, n_modes, n_modes), lambda a: (a, 0, 0)),
        ],
        out_specs=pl.BlockSpec((v_parts, 1, n_bands * r, cols), lambda a: (0, a, 0, 0)),
        out_shape=jax.ShapeDtypeStruct((v_parts, q, n_bands * r, cols), BF16),
        compiler_params=VMEM,
        name="rotate_modes",
    )(coupling, rotation)


def main_kernel(
    n_bands, n_v, r, group,
    freq_ref, a_ref, eig_ref, en_ref, lim_ref, idx_ref, phase_ref,
    el_out, ph_out,
    a_scr, v_scr, u_scr, ek_scr, ep_scr, lk_scr, lp_scr, w_scr, t_scr, el_scr, ph_scr,
):
    m = pl.program_id(0)
    n_src = a_ref.shape[0]
    depth = n_bands * r
    k_all = eig_ref.shape[0]
    k_loc = idx_ref.shape[1]
    high = lax.Precision.HIGHEST
    tn = (((0,), (0,)), ((), ()))

    @pl.when(m == 0)
    def _():
        for s in range(n_src):
            a_scr[:, s * depth : (s + 1) * depth] = a_ref[s].astype(F32).T.astype(BF16)
        at = iota((k_all, k_loc), 0)
        own = at == idx_ref[0:1, :]
        far = at == idx_ref[1:2, :]
        own_b, far_b = own.astype(BF16), far.astype(BF16)
        own_f, far_f = own.astype(F32), far.astype(F32)
        u_scr[...] = lax.dot_general(eig_ref[...], own_b, tn, preferred_element_type=F32).reshape(
            n_bands, n_bands, k_loc
        )
        v_scr[...] = lax.dot_general(eig_ref[...], far_b, tn, preferred_element_type=F32).reshape(
            n_bands, n_bands, k_loc
        )
        en = en_ref[...]
        ek_scr[...] = lax.dot_general(en, own_f, tn, precision=high, preferred_element_type=F32)
        ep_scr[...] = lax.dot_general(en, far_f, tn, precision=high, preferred_element_type=F32)
        lim = lim_ref[...]
        lk_scr[...] = jnp.dot(lim, own_f, precision=high, preferred_element_type=F32)
        lp_scr[...] = jnp.dot(lim, far_f, precision=high, preferred_element_type=F32)
        el_scr[...] = jnp.zeros_like(el_scr)
        ph_scr[...] = jnp.zeros_like(ph_scr)

    ph = phase_ref[...].astype(F32)
    for i in range(0, n_bands, 2):
        v0 = v_scr[i, pl.ds(m, 1), :]
        v1 = v_scr[i + 1, pl.ds(m, 1), :]
        for s in range(n_src):
            p = ph[s * r : (s + 1) * r, :]
            w_scr[s * depth + i * r : s * depth + (i + 2) * r, :] = jnp.concatenate(
                [p * v0, p * v1], axis=0
            ).astype(BF16)
    t_scr[...] = jnp.dot(a_scr[...], w_scr[...], preferred_element_type=F32)

    norm = 1.0 / (math.sqrt(2.0 * math.pi) * SIGMA)
    ep = ep_scr[pl.ds(m, 1), :]
    ek = ek_scr[...]
    base = ep - ek
    mask_m = jnp.where(m.astype(F32) < lp_scr[0:1, :], norm, 0.0)
    mask = jnp.where(iota((n_bands, k_loc), 0).astype(F32) < lk_scr[0:1, :], mask_m, 0.0)
    occ = jax.nn.sigmoid(-ek / THERMAL_ENERGY_KT) - jax.nn.sigmoid(-ep / THERMAL_ENERGY_KT)
    el = el_scr[...]
    for g in range(0, n_v, group):
        vs = range(g, min(g + group, n_v))
        acc = [None] * len(vs)
        for j in range(n_bands):
            u = u_scr[j]
            for x, v in enumerate(vs):
                term = t_scr[v * n_bands + j : v * n_bands + j + 1, :] * u
                acc[x] = term if acc[x] is None else acc[x] + term
        for x, v in enumerate(vs):
            diff = base - freq_ref[0, v]
            strength = acc[x] * acc[x] * jnp.exp(diff * diff * (-0.5 / (SIGMA * SIGMA))) * mask
            el = el + strength
            ph_scr[v] += strength * occ
    el_scr[...] = el

    @pl.when(m == pl.num_programs(0) - 1)
    def _():
        el_out[...] = el_scr[...]
        ph_out[...] = jnp.sum(jnp.sum(ph_scr[...], axis=1), axis=1, keepdims=True)


def linewidths(freq, a, eig, energies, limits, index, phase, n_bands, r):
    n_src, depth, cols = a.shape
    n_v = cols // n_bands
    k_loc = index.shape[1]
    total = n_src * depth
    whole = lambda *s: pl.BlockSpec(s, lambda m: (0,) * len(s))
    return pl.pallas_call(
        functools.partial(main_kernel, n_bands, n_v, r, 3),
        grid=(n_bands,),
        in_specs=[
            pl.BlockSpec(memory_space=pltpu.SMEM),
            whole(*a.shape),
            whole(*eig.shape),
            whole(*energies.shape),
            whole(*limits.shape),
            whole(*index.shape),
            whole(*phase.shape),
        ],
        out_specs=[whole(n_bands, k_loc), whole(n_v, 1)],
        out_shape=[
            jax.ShapeDtypeStruct((n_bands, k_loc), F32),
            jax.ShapeDtypeStruct((n_v, 1), F32),
        ],
        scratch_shapes=[
            pltpu.VMEM((cols, total), BF16),
            pltpu.VMEM((n_bands, n_bands, k_loc), F32),
            pltpu.VMEM((n_bands, n_bands, k_loc), F32),
            pltpu.VMEM((n_bands, k_loc), F32),
            pltpu.VMEM((n_bands, k_loc), F32),
            pltpu.VMEM((1, k_loc), F32),
            pltpu.VMEM((1, k_loc), F32),
            pltpu.VMEM((total, k_loc), BF16),
            pltpu.VMEM((cols, k_loc), F32),
            pltpu.VMEM((n_bands, k_loc), F32),
            pltpu.VMEM((n_v, n_bands, k_loc), F32),
        ],
        compiler_params=VMEM,
        name="linewidths",
    )(freq, a, eig, energies, limits, index, phase)


def on_device(coupling, rotation, freq, eigvec, energies, window, kq_index, kpoints, lattice):
    plane = ("ka", "row")
    everywhere = ("ka", "pb", "row")
    n_ka = lax.axis_size("ka")
    n_row = lax.axis_size("row")
    n_pb = lax.axis_size("pb")
    n_group = n_ka * n_row
    k_dev, n_bands = eigvec.shape[:2]
    q_dev, n_modes = rotation.shape[:2]
    assert q_dev == n_row
    total_k = k_dev * n_group
    total_q = q_dev * n_pb
    v_parts = math.gcd(n_modes, n_ka)
    k_parts = n_ka // v_parts
    v_count = n_modes // v_parts
    k_loc = total_k // k_parts
    ka_pos = lax.axis_index("ka")
    row_pos = lax.axis_index("row")
    pb_pos = lax.axis_index("pb")

    eig_all = lax.all_gather(eigvec.reshape(k_dev, n_bands * n_bands), plane, axis=0, tiled=True)
    level = jnp.concatenate([energies, window.astype(F32)[:, None]], axis=1)
    level_all = lax.all_gather(level, plane, axis=0, tiled=True)

    pad = -coupling.shape[1] % 8
    phase_lat = lattice
    if pad:
        coupling = jnp.pad(coupling, ((0, 0), (0, pad), (0, 0)))
    r = coupling.shape[1]
    rotated = rotate(coupling, rotation, n_bands, v_parts)
    if k_parts > 1:
        rotated = jnp.repeat(rotated, k_parts, axis=0)
    rotated = rotated.reshape((n_group,) + rotated.shape[2:])
    a = lax.all_to_all(rotated, plane, 0, 0, tiled=True)

    k_start = (ka_pos % k_parts) * k_loc
    kp = lax.dynamic_slice_in_dim(kpoints, k_start, k_loc, 0)
    phase = phase_table(phase_lat, kp)
    if pad:
        phase = jnp.pad(phase.reshape(n_group, r - pad, k_loc), ((0, 0), (0, pad), (0, 0)))
        phase = phase.reshape(n_group * r, k_loc)
    kq = lax.dynamic_slice(kq_index, (row_pos, k_start), (1, k_loc))
    index = jnp.concatenate([jnp.arange(k_loc, dtype=jnp.int32)[None] + k_start, kq], axis=0)
    v_start = (ka_pos // k_parts) * v_count
    freq_mine = lax.dynamic_slice(freq, (row_pos, v_start), (1, v_count))
    el, ph = linewidths(
        freq_mine, a, eig_all, level_all[:, :n_bands], level_all[:, n_bands:].T, index, phase,
        n_bands, r,
    )
    el = el * (1.0 / (total_q * n_modes * n_bands))
    ph = ph[:, 0] * (1.0 / (total_k * n_bands))
    if k_parts > 1:
        el = lax.dynamic_update_slice(jnp.zeros((n_bands, total_k), F32), el, (jnp.int32(0), k_start))
    per_row = 128 // k_dev
    fold = n_bands // per_row
    el = el.reshape(per_row, fold, n_group, k_dev).transpose(2, 1, 0, 3).reshape(n_group, fold, 128)
    ph_rows = 8 - fold % 8
    ph = jnp.pad(ph, (0, ph_rows * 128 - v_count)).reshape(1, ph_rows, 128)
    send = jnp.concatenate([el, jnp.broadcast_to(ph, (n_group, ph_rows, 128))], axis=1)
    send = send.reshape(n_ka, 1, n_row, fold + ph_rows, 128)
    send = jnp.broadcast_to(send, (n_ka, n_pb, n_row, fold + ph_rows, 128))
    send = send.reshape(n_group * n_pb, fold + ph_rows, 128)
    got = lax.all_to_all(send, everywhere, 0, 0, tiled=True)
    got = got.reshape(n_ka, n_pb, n_row, fold + ph_rows, 128)
    electron = jnp.sum(got[:, :, :, :fold], axis=(0, 1, 2))
    electron = electron.reshape(fold, per_row, k_dev).transpose(2, 1, 0).reshape(k_dev, n_bands)
    near = lax.dynamic_index_in_dim(got, pb_pos, 1, keepdims=False)[:, :, fold, :v_count]
    near = near.reshape(v_parts, k_parts, n_row, v_count).sum(axis=1)
    phonon = near.transpose(1, 0, 2).reshape(n_row, n_modes)
    return (electron, phonon)


def solution(mesh):
    return jax.shard_map(
        on_device,
        mesh=mesh,
        in_specs=(
            P("pb", ("ka", "row"), None),
            P("pb", None, None),
            P("pb", None),
            P(("ka", "row"), None, None),
            P(("ka", "row"), None),
            P(("ka", "row")),
            P("pb", None),
            P(),
            P(),
        ),
        out_specs=(P(("ka", "row"), None), P("pb", None)),
        check_vma=False,
    )
```

```python
import functools
import math

import jax
import jax.numpy as jnp
import numpy as np
from jax import lax
from jax.experimental import pallas as pl
from jax.experimental.pallas import tpu as pltpu
from jax.sharding import PartitionSpec as P

SIGMA = 0.1
THERMAL_ENERGY_KT = 0.2
VMEM = pltpu.CompilerParams(vmem_limit_bytes=56 * 1024 * 1024)
F32 = jnp.float32
BF16 = jnp.bfloat16


def phase_table(lattice, kpoint_rows):
    rvec = lattice.astype(jnp.float32)
    argument = (
        rvec[:, 0:1] * kpoint_rows[:, 0][None, :]
        + rvec[:, 1:2] * kpoint_rows[:, 1][None, :]
        + rvec[:, 2:3] * kpoint_rows[:, 2][None, :]
    )
    return jnp.cos(2.0 * math.pi * argument).astype(jnp.bfloat16)


def iota(shape, dim):
    return lax.broadcasted_iota(jnp.int32, shape, dim)


def rotate_kernel(n_modes, n_bands, v_parts, halves, coup_ref, rot_ref, out_ref):
    r = coup_ref.shape[1]
    pair = n_bands * n_bands
    rows = n_modes * r
    x = coup_ref[0].astype(F32)
    x = jnp.concatenate([x[:, c * pair : (c + 1) * pair] for c in range(n_modes)], axis=0).astype(BF16)
    rot = rot_ref[0]
    spread_v = (iota((rows, n_modes), 0) // r == iota((rows, n_modes), 1)).astype(BF16)
    spread_c = (iota((n_modes, rows), 1) // r == iota((n_modes, rows), 0)).astype(BF16)
    half = lax.dot_general(spread_v, rot, (((1,), (1,)), ((), ())), preferred_element_type=F32)
    full = jnp.dot(half.astype(BF16), spread_c, preferred_element_type=F32)
    same = iota((rows, rows), 0) % r == iota((rows, rows), 1) % r
    big = jnp.where(same, full, 0.0).astype(BF16)
    y = jnp.dot(big, x, preferred_element_type=F32)
    v_each = n_modes // v_parts // halves
    cols = v_each * n_bands
    for part in range(v_parts):
        pieces = []
        for h in range(halves):
            first = (part * halves + h) * v_each
            for i in range(n_bands):
                block = [
                    y[v * r : (v + 1) * r, i * n_bands : (i + 1) * n_bands]
                    for v in range(first, first + v_each)
                ]
                if cols % 128:
                    block.append(jnp.zeros((r, -cols % 128), F32))
                pieces.append(jnp.concatenate(block, axis=1))
        out_ref[part, 0] = jnp.concatenate(pieces, axis=0).T[:cols].astype(BF16)


def rotate(coupling, rotation, n_bands, v_parts, halves):
    q, r, width = coupling.shape
    n_modes = rotation.shape[1]
    rows = n_modes // v_parts // halves * n_bands
    cols = halves * n_bands * r
    return pl.pallas_call(
        functools.partial(rotate_kernel, n_modes, n_bands, v_parts, halves),
        grid=(q,),
        in_specs=[
            pl.BlockSpec((1, r, width), lambda a: (a, 0, 0)),
            pl.BlockSpec((1, n_modes, n_modes), lambda a: (a, 0, 0)),
        ],
        out_specs=pl.BlockSpec((v_parts, 1, rows, cols), lambda a: (0, a, 0, 0)),
        out_shape=jax.ShapeDtypeStruct((v_parts, q, rows, cols), BF16),
        compiler_params=VMEM,
        name="rotate_modes",
    )(coupling, rotation)


def prepare_kernel(
    n_bands, n_v,
    freq_ref, start_ref, kq_ref, points_ref, phase_ref,
    pv_out, bd_out, eo_out, so_out,
    eig_scr, en_scr, fl_scr,
):
    g = pl.program_id(0)
    per = 128 // n_bands
    k_all = points_ref.shape[0]
    k_loc = phase_ref.shape[1]
    n_r = phase_ref.shape[0]
    at_once = pv_out.shape[0]
    at_en = points_ref.shape[1] - 128
    n_vg = fl_scr.shape[1] // 128
    scale = 1.0 / (SIGMA * math.sqrt(2.0))
    lane = iota((1, 128), 1)
    roll = lambda x, shift: pltpu.roll(x, shift % 128, 1) if shift % 128 else x

    @pl.when(g == 0)
    def _():
        en = points_ref[:, at_en:].astype(F32)
        lim = en[:, 3 * n_bands : 3 * n_bands + 1]
        level = en + roll(en, -n_bands) + roll(en, -2 * n_bands)
        en_scr[...] = jnp.where(lane < n_bands, level, 0.0)
        keep = lane.astype(F32) < jnp.minimum(lim, float(n_bands))
        for i in range(n_bands):
            lo = i * n_bands
            tile = lo // 128 * 128
            block = roll(points_ref[:, tile : tile + 128].astype(F32), tile - lo)
            if lo + n_bands > tile + 128:
                more = roll(points_ref[:, tile + 128 : tile + 256].astype(F32), tile - lo)
                block = jnp.where(lane < tile + 128 - lo, block, more)
            eig_scr[pl.ds(i, k_all, stride=n_bands), :] = jnp.where(keep, block, 0.0)
        for vg in range(n_vg):
            row = jnp.zeros((1, 128), F32)
            for x in range(min(per, n_v - vg * per)):
                row = jnp.where(lane // n_bands == x, freq_ref[0, vg * per + x], row)
            fl_scr[0:1, vg * 128 : (vg + 1) * 128] = row

    for t in range(at_once):
        first = (g * at_once + t) * 2 * per
        c = iota((1, 256), 1)
        k_lane = first + c // 128 * per + c % 128 // n_bands
        k_lane = jnp.where((c % 128 < per * n_bands) & (k_lane < k_loc), k_lane, -1)
        spread = (iota((k_loc, 256), 0) == k_lane).astype(BF16)
        pv_out[t, :n_r, :] = jnp.dot(phase_ref[...], spread, preferred_element_type=F32).astype(BF16)
        far_rows = []
        v_tiles = []
        for kg in range(2):
            vl = None
            level = None
            diagonal = []
            for x in range(per):
                k = jnp.minimum(first + kg * per + x, k_loc - 1)
                near = k + start_ref[0]
                far = kq_ref[0, k]
                v = roll(eig_scr[pl.ds(pl.multiple_of(far * n_bands, 8), n_bands), :], n_bands * x)
                u = roll(eig_scr[pl.ds(pl.multiple_of(near * n_bands, 8), n_bands), :], n_bands * x)
                e = roll(en_scr[pl.ds(near, 1), :], n_bands * x)
                vl = v if vl is None else vl + v
                level = e if level is None else level + e
                diagonal.append(u)
                far_rows.append(en_scr[pl.ds(far, 1), :])
            v_tiles.append(vl)
            diagonal.append(jnp.zeros((128 - per * n_bands, 128), F32))
            bd_out[t, kg] = jnp.concatenate(diagonal, axis=0).T.astype(BF16)
            rows = slice(kg * 128, (kg + 1) * 128)
            occ = jax.nn.sigmoid(-level / THERMAL_ENERGY_KT)
            eo_out[t, rows, :128] = jnp.broadcast_to(level * scale, (128, 128)).T
            eo_out[t, rows, 128:] = jnp.broadcast_to(occ, (128, 128)).T
        pv_out[t, n_r:, :] = jnp.concatenate(v_tiles, axis=1).astype(BF16)
        far_rows.append(jnp.zeros((16 - 2 * per, 128), F32))
        far_e = jnp.concatenate(far_rows, axis=0)
        far_e = sum((roll(far_e, n_bands * x) for x in range(1, per)), far_e)
        so_out[t, :, n_vg * 128 :] = jax.nn.sigmoid(-far_e / THERMAL_ENERGY_KT)
        for vg in range(n_vg):
            sh = (far_e - fl_scr[0:1, vg * 128 : (vg + 1) * 128]) * scale
            so_out[t, :, vg * 128 : (vg + 1) * 128] = jnp.where(lane < per * n_bands, sh, 1e4)


def prepare(freq, start, kq, points, phase, n_bands, n_v, at_once=4):
    per = 128 // n_bands
    k_loc = phase.shape[1]
    tiles = -(-k_loc // (2 * per * at_once)) * at_once
    n_vg = -(-n_v // per)
    k_all = points.shape[0]
    n_pv = phase.shape[0] + n_bands
    whole = lambda x: pl.BlockSpec(x.shape, lambda g: (0,) * x.ndim)
    smem = pl.BlockSpec(memory_space=pltpu.SMEM)
    return pl.pallas_call(
        functools.partial(prepare_kernel, n_bands, n_v),
        grid=(tiles // at_once,),
        in_specs=[smem, smem, smem, whole(points), whole(phase)],
        out_specs=[
            pl.BlockSpec((at_once, n_pv, 256), lambda g: (g, 0, 0)),
            pl.BlockSpec((at_once, 2, 128, 128), lambda g: (g, 0, 0, 0)),
            pl.BlockSpec((at_once, 256, 256), lambda g: (g, 0, 0)),
            pl.BlockSpec((at_once, 16, (n_vg + 1) * 128), lambda g: (g, 0, 0)),
        ],
        out_shape=[
            jax.ShapeDtypeStruct((tiles, n_pv, 256), BF16),
            jax.ShapeDtypeStruct((tiles, 2, 128, 128), BF16),
            jax.ShapeDtypeStruct((tiles, 256, 256), F32),
            jax.ShapeDtypeStruct((tiles, 16, (n_vg + 1) * 128), F32),
        ],
        scratch_shapes=[
            pltpu.VMEM((k_all * n_bands, 128), F32),
            pltpu.VMEM((k_all, 128), F32),
            pltpu.VMEM((1, n_vg * 128), F32),
        ],
        compiler_params=VMEM,
        name="prepare",
    )(freq, start, kq, points, phase)


def lane_ranges(n_bands):
    per = 128 // n_bands
    lane = iota((n_bands, 128), 1)
    inside = []
    for d in range(2 * per - 1):
        lo = n_bands * d % 128
        hi = lo + n_bands
        inside.append(
            (lane >= lo) & (lane < hi) if hi <= 128 else (lane >= lo) | (lane < hi - 128)
        )
    return inside


def swap_blocks(t_ref, kg, n_bands, n_v):
    per = 128 // n_bands
    inside = lane_ranges(n_bands)
    tiles = []
    for first in range(0, n_v, per):
        count = min(per, n_v - first)
        rolled = []
        for x in range(count):
            v = first + x
            block = t_ref[v * n_bands : (v + 1) * n_bands, kg * 128 : (kg + 1) * 128]
            rolled.append(pltpu.roll(block, n_bands * x, 1) if x else block)
        column = []
        for k in range(per):
            mix = rolled[0] if count == per else jnp.where(inside[k], rolled[0], 0.0)
            for x in range(1, count):
                mix = jnp.where(inside[k + x], rolled[x], mix)
            column.append(pltpu.roll(mix, 128 - n_bands * k, 1) if k else mix)
        column.append(jnp.zeros((128 - per * n_bands, 128), F32))
        tiles.append(jnp.concatenate(column, axis=0).astype(BF16))
    return jnp.concatenate(tiles, axis=1)


def fill_products(w_ref, pv, n_bands, r):
    n_src = (pv.shape[0] - n_bands) // r
    depth = n_bands * r
    ph, vl = pv[: n_src * r].astype(F32), pv[n_src * r :].astype(F32)
    if r % 8 == 0:
        for i in range(0, n_bands, 2):
            v0 = vl[i : i + 1, :]
            v1 = vl[i + 1 : i + 2, :]
            for s in range(n_src):
                p = ph[s * r : (s + 1) * r, :]
                at = s * depth + i * r
                w_ref[at : at + 2 * r, :] = jnp.concatenate([p * v0, p * v1], axis=0).astype(BF16)
        return
    row = iota((depth, 1), 0)
    by_band = (row // r == iota((depth, n_bands), 1)).astype(BF16)
    v_rows = jnp.dot(by_band, vl.astype(BF16), preferred_element_type=F32)
    for s in range(n_src):
        by_src = (row % r + s * r == iota((depth, n_src * r), 1)).astype(BF16)
        p_rows = jnp.dot(by_src, ph.astype(BF16), preferred_element_type=F32)
        w_ref[s * depth : (s + 1) * depth, :] = (p_rows * v_rows).astype(BF16)


def group_sums(coupled, kg, eo_ref, so_ref, n_bands, ph):
    per = 128 // n_bands
    n_vg = len(ph)
    sums = []
    for k in range(per):
        here = slice(k * n_bands, (k + 1) * n_bands)
        lo = kg * 128 + k * n_bands
        kk = kg * per + k
        ek = eo_ref[0, lo : lo + n_bands, :128]
        occ = eo_ref[0, lo : lo + n_bands, 128:] - so_ref[0, kk : kk + 1, n_vg * 128 :]
        el = None
        for vg in range(n_vg):
            c = coupled[here, vg * 128 : (vg + 1) * 128]
            d = so_ref[0, kk : kk + 1, vg * 128 : (vg + 1) * 128] - ek
            strength = c * c * jnp.exp(-(d * d))
            el = strength if el is None else el + strength
            weighed = strength * occ
            ph[vg] = weighed if ph[vg] is None else ph[vg] + weighed
        sums.append(el)
    sums.append(jnp.zeros((128 - per * n_bands, 128), F32))
    return jnp.sum(jnp.concatenate(sums, axis=0).T, axis=0, keepdims=True)


def product_and_sums(a_ref, w_ref, t_new, t_old, bd_ref, eo_ref, so_ref, n_bands, n_v):
    per = 128 // n_bands
    n_vg = -(-n_v // per)
    cuts = [min(x * per, n_v) * n_bands for x in range(n_vg + 1)]
    parts = [slice(a, b) for a, b in zip(cuts, cuts[1:])]
    parts += [slice(0, 0)] * (4 - n_vg)

    def product(x):
        if parts[x].stop > parts[x].start:
            t_new[parts[x], :] = jnp.dot(a_ref[parts[x], :], w_ref[...], preferred_element_type=F32)

    ph = [None] * n_vg
    product(0)
    right = swap_blocks(t_old, 0, n_bands, n_v)
    product(1)
    c0 = jnp.dot(bd_ref[0, 0], right, preferred_element_type=F32)
    right = swap_blocks(t_old, 1, n_bands, n_v)
    product(2)
    el0 = group_sums(c0, 0, eo_ref, so_ref, n_bands, ph)
    c1 = jnp.dot(bd_ref[0, 1], right, preferred_element_type=F32)
    product(3)
    el1 = group_sums(c1, 1, eo_ref, so_ref, n_bands, ph)
    for x in range(4, n_vg):
        product(x)
    return [el0, el1], ph


def linewidth_kernel(
    n_bands, n_v, halves, r, el_scale, ph_scale,
    a_ref, pv_ref, bd0_ref, bd1_ref, eo0_ref, eo1_ref, so0_ref, so1_ref,
    el_out, ph_out,
    a_scr, w0_scr, w1_scr, t0_scr, t1_scr, ph_scr,
):
    g = pl.program_id(0)
    last = pl.num_programs(0) - 1
    n_src, rows, wide = a_ref.shape
    depth = wide // halves
    n_vg = ph_scr.shape[0]

    @pl.when(g == 0)
    def _():
        for s in range(n_src):
            block = a_ref[s]
            for h in range(halves):
                a_scr[h * rows : (h + 1) * rows, s * depth : (s + 1) * depth] = block[
                    :, h * depth : (h + 1) * depth
                ]
        t1_scr[...] = jnp.zeros_like(t1_scr)
        ph_scr[...] = jnp.zeros_like(ph_scr)

    fill_products(w0_scr, pv_ref[0], n_bands, r)
    el0, ph0 = product_and_sums(
        a_scr, w0_scr, t0_scr, t1_scr, bd0_ref, eo0_ref, so0_ref, n_bands, n_v
    )
    fill_products(w1_scr, pv_ref[1], n_bands, r)
    el1, ph1 = product_and_sums(
        a_scr, w1_scr, t1_scr, t0_scr, bd1_ref, eo1_ref, so1_ref, n_bands, n_v
    )
    el_out[g] = jnp.concatenate(el0 + el1, axis=0) * el_scale
    second = jnp.where(g < last, 1.0, 0.0)
    for vg in range(n_vg):
        ph_scr[vg] += ph0[vg] + ph1[vg] * second

    @pl.when(g == last)
    def _():
        fold = (iota((128, 128), 0) // n_bands == iota((128, 128), 1)).astype(F32)
        sums = jnp.sum(ph_scr[...], axis=1)
        ph_out[...] = (
            jnp.dot(sums, fold, precision=lax.Precision.HIGHEST, preferred_element_type=F32) * ph_scale
        )


def linewidths(a, prepared, k_loc, n_bands, n_v, halves, r, el_scale, ph_scale):
    pv, bd, eo, so = prepared
    steps = -(-k_loc // (128 // n_bands * 4))
    n_vg = so.shape[2] // 128 - 1
    total = (pv.shape[1] - n_bands) * n_bands
    tile0 = lambda g: jnp.maximum(2 * g - 1, 0)
    tile1 = lambda g: jnp.minimum(2 * g, 2 * steps - 1)
    pairs = [
        pl.BlockSpec((1,) + x.shape[1:], lambda g, f=f, n=x.ndim: (f(g),) + (0,) * (n - 1))
        for x in (bd, eo, so)
        for f in (tile0, tile1)
    ]
    el, ph = pl.pallas_call(
        functools.partial(linewidth_kernel, n_bands, n_v, halves, r, el_scale, ph_scale),
        grid=(steps + 1,),
        in_specs=[
            pl.BlockSpec(a.shape, lambda g: (0, 0, 0)),
            pl.BlockSpec((2,) + pv.shape[1:], lambda g: (jnp.minimum(g, steps - 1), 0, 0)),
        ]
        + pairs,
        out_specs=[
            pl.BlockSpec((steps + 1, 4, 128), lambda g: (0, 0, 0)),
            pl.BlockSpec((n_vg, 128), lambda g: (0, 0)),
        ],
        out_shape=[
            jax.ShapeDtypeStruct((steps + 1, 4, 128), F32),
            jax.ShapeDtypeStruct((n_vg, 128), F32),
        ],
        scratch_shapes=[
            pltpu.VMEM((n_v * n_bands, total), BF16),
            pltpu.VMEM((total, 256), BF16),
            pltpu.VMEM((total, 256), BF16),
            pltpu.VMEM((n_v * n_bands, 256), F32),
            pltpu.VMEM((n_v * n_bands, 256), F32),
            pltpu.VMEM((n_vg, n_bands, 128), F32),
        ],
        compiler_params=VMEM,
        name="linewidths",
    )(a, pv, bd, bd, eo, eo, so, so)
    return el.reshape(-1, 128)[2:], ph


def on_device(coupling, rotation, freq, eigvec, energies, window, kq_index, kpoints, lattice):
    plane = ("ka", "row")
    everywhere = ("ka", "pb", "row")
    n_ka = lax.axis_size("ka")
    n_row = lax.axis_size("row")
    n_pb = lax.axis_size("pb")
    n_group = n_ka * n_row
    k_dev, n_bands = eigvec.shape[:2]
    q_dev, n_modes = rotation.shape[:2]
    assert q_dev == n_row
    pair = n_bands * n_bands
    total_k = k_dev * n_group
    total_q = q_dev * n_pb
    v_parts = math.gcd(n_modes, n_ka)
    k_parts = n_ka // v_parts
    n_v = n_modes // v_parts
    halves = 2 if n_v % 2 == 0 else 1
    k_loc = total_k // k_parts
    ka_pos = lax.axis_index("ka")
    row_pos = lax.axis_index("row")
    pb_pos = lax.axis_index("pb")

    parts, rest = [], energies
    for _ in range(3):
        part = lax.reduce_precision(rest, 8, 7)
        parts.append(part.astype(BF16))
        rest = rest - part
    gap = -pair % 128
    mine = [eigvec.reshape(k_dev, pair), jnp.zeros((k_dev, gap), BF16)] + parts
    mine += [window.astype(BF16)[:, None], jnp.zeros((k_dev, 127 - 3 * n_bands), BF16)]
    mine = jnp.concatenate(mine, axis=1)
    points = lax.all_to_all(
        jnp.broadcast_to(mine[None], (n_group,) + mine.shape), plane, 0, 0, tiled=True
    ).reshape(total_k, mine.shape[1])

    pad = -coupling.shape[1] % 8
    if pad:
        coupling = jnp.pad(coupling, ((0, 0), (0, pad), (0, 0)))
    r, r_sent = coupling.shape[1] - pad, coupling.shape[1]
    rotated = rotate(coupling, rotation, n_bands, v_parts, halves)
    if k_parts > 1:
        rotated = jnp.repeat(rotated, k_parts, axis=0)
    rotated = rotated.reshape((n_group,) + rotated.shape[2:])
    a = lax.all_to_all(rotated, plane, 0, 0, tiled=True)
    if pad:
        a = a.reshape(a.shape[:2] + (halves * n_bands, r_sent))[..., :r]
        a = a.reshape(a.shape[:2] + (halves * n_bands * r,))

    k_start = (ka_pos % k_parts) * k_loc
    kp = lax.dynamic_slice_in_dim(kpoints, k_start, k_loc, 0)
    phase = phase_table(lattice, kp)
    kq = lax.dynamic_slice(kq_index, (row_pos, k_start), (1, k_loc))
    v_start = (ka_pos // k_parts) * n_v
    freq_mine = lax.dynamic_slice(freq, (row_pos, v_start), (1, n_v))
    prepared = prepare(
        freq_mine, k_start[None], kq, points, phase, n_bands, n_v
    )
    norm = 1.0 / (math.sqrt(2.0 * math.pi) * SIGMA)
    el, ph = linewidths(
        a, prepared, k_loc, n_bands, n_v, halves, r,
        norm / (total_q * n_modes * n_bands), norm / (total_k * n_bands),
    )
    per = 128 // n_bands
    el = el[:, : per * n_bands].reshape(-1, n_bands)[:k_loc].T
    ph = ph[:, :per].reshape(-1)[:n_v]
    if k_parts > 1:
        el = lax.dynamic_update_slice(jnp.zeros((n_bands, total_k), F32), el, (jnp.int32(0), k_start))
    per_row = 128 // k_dev
    fold = n_bands // per_row
    el = el.reshape(per_row, fold, n_group, k_dev).transpose(2, 1, 0, 3).reshape(n_group, fold, 128)
    ph_rows = 8 - fold % 8
    ph = jnp.pad(ph, (0, ph_rows * 128 - n_v)).reshape(1, ph_rows, 128)
    send = jnp.concatenate([el, jnp.broadcast_to(ph, (n_group, ph_rows, 128))], axis=1)
    send = send.reshape(n_ka, 1, n_row, fold + ph_rows, 128)
    send = jnp.broadcast_to(send, (n_ka, n_pb, n_row, fold + ph_rows, 128))
    send = send.reshape(n_group * n_pb, fold + ph_rows, 128)
    got = lax.all_to_all(send, everywhere, 0, 0, tiled=True)
    got = got.reshape(n_ka, n_pb, n_row, fold + ph_rows, 128)
    electron = jnp.sum(got[:, :, :, :fold], axis=(0, 1, 2))
    electron = electron.reshape(fold, per_row, k_dev).transpose(2, 1, 0).reshape(k_dev, n_bands)
    near = lax.dynamic_index_in_dim(got, pb_pos, 1, keepdims=False)[:, :, fold, :n_v]
    near = near.reshape(v_parts, k_parts, n_row, n_v).sum(axis=1)
    phonon = near.transpose(1, 0, 2).reshape(n_row, n_modes)
    return (electron, phonon)


def solution(mesh):
    return jax.shard_map(
        on_device,
        mesh=mesh,
        in_specs=(
            P("pb", ("ka", "row"), None),
            P("pb", None, None),
            P("pb", None),
            P(("ka", "row"), None, None),
            P(("ka", "row"), None),
            P(("ka", "row")),
            P("pb", None),
            P(),
            P(),
        ),
        out_specs=(P(("ka", "row"), None), P("pb", None)),
        check_vma=False,
    )
```

```python
import functools
import math

import jax
import jax.numpy as jnp
import numpy as np
from jax import lax
from jax.experimental import pallas as pl
from jax.experimental.pallas import tpu as pltpu
from jax.sharding import PartitionSpec as P

SIGMA = 0.1
THERMAL_ENERGY_KT = 0.2
VMEM = pltpu.CompilerParams(vmem_limit_bytes=40 * 1024 * 1024)
F32 = jnp.float32
BF16 = jnp.bfloat16
UNROLL = 3


def phase_table(lattice, kpoint_rows):
    rvec = lattice.astype(jnp.float32)
    argument = (
        rvec[:, 0:1] * kpoint_rows[:, 0][None, :]
        + rvec[:, 1:2] * kpoint_rows[:, 1][None, :]
        + rvec[:, 2:3] * kpoint_rows[:, 2][None, :]
    )
    return jnp.cos(2.0 * math.pi * argument).astype(jnp.bfloat16)


def iota(shape, dim):
    return lax.broadcasted_iota(jnp.int32, shape, dim)


def pack_kernel(eig_ref, en_ref, window_ref, out_ref):
    n_bands, _, k_dev = eig_ref.shape
    pair = n_bands * n_bands
    rows = [eig_ref[...].astype(F32).reshape(pair, k_dev), jnp.zeros((-pair % 128, k_dev), F32)]
    rest = en_ref[...]
    for _ in range(3):
        part = rest.astype(BF16).astype(F32)
        rows.append(part)
        rest = rest - part
    rows.append(window_ref[...].astype(F32))
    rows.append(jnp.zeros((127 - 3 * n_bands, k_dev), F32))
    packed = jnp.concatenate(rows, axis=0)
    packed = jnp.concatenate([packed, jnp.zeros((packed.shape[0], 128 - k_dev), F32)], axis=1)
    packed = packed.T[:k_dev].astype(BF16)
    for d in range(out_ref.shape[0]):
        out_ref[d] = packed


def pack(eigvec, energies, window, copies):
    k_dev, n_bands, _ = eigvec.shape
    wide = -(-n_bands * n_bands // 128) * 128 + 128
    args = (eigvec.transpose(1, 2, 0), energies.T, window.reshape(1, k_dev))
    return pl.pallas_call(
        pack_kernel,
        grid=(1,),
        in_specs=[pl.BlockSpec(x.shape, lambda g, n=x.ndim: (0,) * n) for x in args],
        out_specs=pl.BlockSpec((copies, k_dev, wide), lambda g: (0, 0, 0)),
        out_shape=jax.ShapeDtypeStruct((copies, k_dev, wide), BF16),
        compiler_params=VMEM,
        name="pack_points",
    )(*[pltpu.with_memory_space_constraint(x, pltpu.HBM) for x in args])


def finish_kernel(n_bands, n_v, k_parts, place_ref, got_ref, el_out, ph_out, scr):
    per = 128 // n_bands
    n_ka, n_pb, n_row, rows, _ = got_ref.shape
    lane = iota((1, 128), 1)
    total = None
    for ka in range(n_ka):
        for pb in range(n_pb):
            for row in range(n_row):
                part = got_ref[ka, pb, row]
                total = part if total is None else total + part
    for x in range(per):
        shifted = pltpu.roll(total, 128 - n_bands * x, 1) if x else total
        scr[pl.ds(x, rows, stride=per), :] = shifted
    k_dev = el_out.shape[1]
    mine = scr[pl.ds(place_ref[1], k_dev), :]
    mine = jnp.concatenate([mine, jnp.zeros((128 - k_dev, 128), F32)], axis=0)
    el_out[...] = mine.T[:n_bands, :k_dev]
    for row in range(n_row):
        line = jnp.zeros((1, 128), F32)
        for ka in range(n_ka):
            part = got_ref[ka, pl.ds(place_ref[0], 1), row][0]
            for first in range(0, n_v, per):
                to = ka // k_parts * n_v + first
                vg = first // per
                moved = pltpu.roll(part[vg : vg + 1], (to - per * n_bands) % 128, 1)
                count = min(per, n_v - first)
                line = line + jnp.where((lane >= to) & (lane < to + count), moved, 0.0)
        ph_out[row : row + 1, :] = line[:, : ph_out.shape[1]]


def finish(got, place, n_bands, n_v, k_parts, k_dev, n_modes):
    n_row, rows = got.shape[2:4]
    per = 128 // n_bands
    el, ph = pl.pallas_call(
        functools.partial(finish_kernel, n_bands, n_v, k_parts),
        in_specs=[pl.BlockSpec(memory_space=pltpu.SMEM), pl.BlockSpec(memory_space=pltpu.VMEM)],
        out_shape=[
            jax.ShapeDtypeStruct((n_bands, k_dev), F32),
            jax.ShapeDtypeStruct((n_row, n_modes), F32),
        ],
        scratch_shapes=[pltpu.VMEM((rows * per, 128), F32)],
        compiler_params=VMEM,
        name="finish",
    )(place, pltpu.with_memory_space_constraint(got, pltpu.VMEM))
    return el.T, ph


def rotate_kernel(n_modes, n_bands, v_parts, halves, coup_ref, rot_ref, out_ref):
    r = coup_ref.shape[1]
    pair = n_bands * n_bands
    rows = n_modes * r
    x = coup_ref[0].astype(F32)
    x = jnp.concatenate([x[:, c * pair : (c + 1) * pair] for c in range(n_modes)], axis=0).astype(BF16)
    rot = rot_ref[0]
    spread_v = (iota((rows, n_modes), 0) // r == iota((rows, n_modes), 1)).astype(BF16)
    spread_c = (iota((n_modes, rows), 1) // r == iota((n_modes, rows), 0)).astype(BF16)
    half = lax.dot_general(spread_v, rot, (((1,), (1,)), ((), ())), preferred_element_type=F32)
    full = jnp.dot(half.astype(BF16), spread_c, preferred_element_type=F32)
    same = iota((rows, rows), 0) % r == iota((rows, rows), 1) % r
    big = jnp.where(same, full, 0.0).astype(BF16)
    y = jnp.dot(big, x, preferred_element_type=F32)
    v_each = n_modes // v_parts // halves
    cols = v_each * n_bands
    for part in range(v_parts):
        pieces = []
        for h in range(halves):
            first = (part * halves + h) * v_each
            for i in range(n_bands):
                block = [
                    y[v * r : (v + 1) * r, i * n_bands : (i + 1) * n_bands]
                    for v in range(first, first + v_each)
                ]
                if cols % 128:
                    block.append(jnp.zeros((r, -cols % 128), F32))
                pieces.append(jnp.concatenate(block, axis=1))
        out_ref[part, 0] = jnp.concatenate(pieces, axis=0).T[:cols].astype(BF16)


def rotate(coupling, rotation, n_bands, v_parts, halves):
    q, r, width = coupling.shape
    n_modes = rotation.shape[1]
    rows = n_modes // v_parts // halves * n_bands
    cols = halves * n_bands * r
    return pl.pallas_call(
        functools.partial(rotate_kernel, n_modes, n_bands, v_parts, halves),
        grid=(q,),
        in_specs=[
            pl.BlockSpec((1, r, width), lambda a: (a, 0, 0)),
            pl.BlockSpec((1, n_modes, n_modes), lambda a: (a, 0, 0)),
        ],
        out_specs=pl.BlockSpec((v_parts, 1, rows, cols), lambda a: (0, a, 0, 0)),
        out_shape=jax.ShapeDtypeStruct((v_parts, q, rows, cols), BF16),
        compiler_params=VMEM,
        name="rotate_modes",
    )(coupling, rotation)


def prepare_kernel(
    n_bands, n_v, at_once,
    freq_ref, start_ref, kq_ref, points_ref, phase_ref,
    pv_out, bd_out, gauss_out, occ_out,
    eig_scr, en_scr, fl_scr,
):
    g = pl.program_id(0)
    per = 128 // n_bands
    k_all = points_ref.shape[0]
    k_loc = phase_ref.shape[1]
    n_r = phase_ref.shape[0]
    at_en = points_ref.shape[1] - 128
    n_vg = fl_scr.shape[1] // 128
    scale = 1.0 / (SIGMA * math.sqrt(2.0))
    lane = iota((1, 128), 1)
    roll = lambda x, shift: pltpu.roll(x, shift % 128, 1) if shift % 128 else x

    @pl.when(g == 0)
    def _():
        en = points_ref[:, at_en:].astype(F32)
        lim = en[:, 3 * n_bands : 3 * n_bands + 1]
        level = en + roll(en, -n_bands) + roll(en, -2 * n_bands)
        en_scr[...] = jnp.where(lane < n_bands, level, 0.0)
        keep = lane.astype(F32) < jnp.minimum(lim, float(n_bands))
        for i in range(n_bands):
            lo = i * n_bands
            tile = lo // 128 * 128
            block = roll(points_ref[:, tile : tile + 128].astype(F32), tile - lo)
            if lo + n_bands > tile + 128:
                more = roll(points_ref[:, tile + 128 : tile + 256].astype(F32), tile - lo)
                block = jnp.where(lane < tile + 128 - lo, block, more)
            eig_scr[pl.ds(i, k_all, stride=n_bands), :] = jnp.where(keep, block, 0.0)
        for vg in range(n_vg):
            row = jnp.zeros((1, 128), F32)
            for x in range(min(per, n_v - vg * per)):
                row = jnp.where(lane // n_bands == x, freq_ref[0, vg * per + x], row)
            fl_scr[0:1, vg * 128 : (vg + 1) * 128] = row

    for step in range(at_once):
        t = g * at_once + step
        first = t * 2 * per
        c = iota((1, 256), 1)
        k_lane = first + c // 128 * per + c % 128 // n_bands
        k_lane = jnp.where((c % 128 < per * n_bands) & (k_lane < k_loc), k_lane, -1)
        spread = (iota((k_loc, 256), 0) == k_lane).astype(BF16)
        pv_out[step, :n_r, :] = jnp.dot(phase_ref[...], spread, preferred_element_type=F32).astype(BF16)
        v_tiles = []
        for kg in range(2):
            vl = None
            level = None
            diagonal = []
            far_rows = []
            for x in range(per):
                k = jnp.minimum(first + kg * per + x, k_loc - 1)
                near = k + start_ref[0]
                far = kq_ref[0, k]
                v = roll(eig_scr[pl.ds(pl.multiple_of(far * n_bands, 8), n_bands), :], n_bands * x)
                u = roll(eig_scr[pl.ds(pl.multiple_of(near * n_bands, 8), n_bands), :], n_bands * x)
                e = roll(en_scr[pl.ds(near, 1), :], n_bands * x)
                vl = v if vl is None else vl + v
                level = e if level is None else level + e
                diagonal.append(u)
                far_rows.append(en_scr[pl.ds(far, 1), :])
            v_tiles.append(vl)
            diagonal.append(jnp.zeros((128 - per * n_bands, 128), F32))
            bd_out[step, kg] = jnp.concatenate(diagonal, axis=0).T.astype(BF16)
            occ = jax.nn.sigmoid(-level / THERMAL_ENERGY_KT)
            near_level = jnp.broadcast_to(level * scale, (128, 128)).T
            near_occ = jnp.broadcast_to(occ, (128, 128)).T
            far_e = jnp.concatenate(far_rows + [jnp.zeros((8 - per, 128), F32)], axis=0)
            far_e = sum((roll(far_e, n_bands * x) for x in range(1, per)), far_e)
            far_occ = jax.nn.sigmoid(-far_e / THERMAL_ENERGY_KT)
            for x in range(per):
                here = slice(x * n_bands, (x + 1) * n_bands)
                rows = slice(kg * 128 + x * n_bands, kg * 128 + (x + 1) * n_bands)
                occ_out[step, rows, :] = near_occ[here] - roll(far_occ[x : x + 1], n_bands * x)
                for vg in range(n_vg):
                    cols = slice(vg * 128, (vg + 1) * 128)
                    sh = (far_e[x : x + 1] - fl_scr[0:1, cols]) * scale
                    sh = roll(jnp.where(lane < per * n_bands, sh, 1e4), n_bands * x)
                    d = sh - near_level[here]
                    gauss_out[step, rows, cols] = jnp.exp(-(d * d)).astype(BF16)
        pv_out[step, n_r:, :] = jnp.concatenate(v_tiles, axis=1).astype(BF16)


def steps_of(k_loc, n_bands):
    tiles = -(-k_loc // (128 // n_bands * 2))
    return tiles, -(-(tiles + 1) // UNROLL)


def prepare(freq, start, kq, points, phase, n_bands, n_v):
    per = 128 // n_bands
    k_loc = phase.shape[1]
    at_once = UNROLL
    tiles = steps_of(k_loc, n_bands)[1] * at_once
    n_vg = -(-n_v // per)
    k_all = points.shape[0]
    n_pv = phase.shape[0] + n_bands
    whole = lambda x: pl.BlockSpec(x.shape, lambda g: (0,) * x.ndim)
    smem = pl.BlockSpec(memory_space=pltpu.SMEM)
    return pl.pallas_call(
        functools.partial(prepare_kernel, n_bands, n_v, at_once),
        grid=(tiles // at_once,),
        in_specs=[smem, smem, smem, pl.BlockSpec(memory_space=pltpu.VMEM), whole(phase)],
        out_specs=[
            pl.BlockSpec((at_once, n_pv, 256), lambda g: (g, 0, 0)),
            pl.BlockSpec((at_once, 2, 128, 128), lambda g: (g, 0, 0, 0)),
            pl.BlockSpec((at_once, 256, n_vg * 128), lambda g: (g, 0, 0)),
            pl.BlockSpec((at_once, 256, 128), lambda g: (g, 0, 0)),
        ],
        out_shape=[
            pltpu.HBM((tiles, n_pv, 256), BF16),
            pltpu.HBM((tiles, 2, 128, 128), BF16),
            pltpu.HBM((tiles, 256, n_vg * 128), BF16),
            pltpu.HBM((tiles, 256, 128), F32),
        ],
        scratch_shapes=[
            pltpu.VMEM((k_all * n_bands, 128), F32),
            pltpu.VMEM((k_all, 128), F32),
            pltpu.VMEM((1, n_vg * 128), F32),
        ],
        compiler_params=VMEM,
        name="prepare",
    )(freq, start, kq, points, phase)


def lane_ranges(n_bands):
    per = 128 // n_bands
    lane = iota((n_bands, 128), 1)
    inside = []
    for d in range(2 * per - 1):
        lo = n_bands * d % 128
        hi = lo + n_bands
        inside.append(
            (lane >= lo) & (lane < hi) if hi <= 128 else (lane >= lo) | (lane < hi - 128)
        )
    return inside


def swap_blocks(t_ref, kg, n_bands, n_v):
    per = 128 // n_bands
    inside = lane_ranges(n_bands)
    tiles = []
    for first in range(0, n_v, per):
        count = min(per, n_v - first)
        rolled = []
        for x in range(count):
            v = first + x
            block = t_ref[v * n_bands : (v + 1) * n_bands, kg * 128 : (kg + 1) * 128]
            rolled.append(pltpu.roll(block, n_bands * x, 1) if x else block)
        column = []
        for k in range(per):
            mix = rolled[0] if count == per else jnp.where(inside[k], rolled[0], 0.0)
            for x in range(1, count):
                mix = jnp.where(inside[k + x], rolled[x], mix)
            column.append(mix)
        column.append(jnp.zeros((128 - per * n_bands, 128), F32))
        tiles.append(jnp.concatenate(column, axis=0).astype(BF16))
    return jnp.concatenate(tiles, axis=1)


def fill_products(w_ref, pv, n_bands, r):
    n_src = (pv.shape[0] - n_bands) // r
    depth = n_bands * r
    ph, vl = pv[: n_src * r].astype(F32), pv[n_src * r :].astype(F32)
    if r % 8 == 0:
        for i in range(0, n_bands, 2):
            v0 = vl[i : i + 1, :]
            v1 = vl[i + 1 : i + 2, :]
            for s in range(n_src):
                p = ph[s * r : (s + 1) * r, :]
                at = s * depth + i * r
                w_ref[at : at + 2 * r, :] = jnp.concatenate([p * v0, p * v1], axis=0).astype(BF16)
        return
    row = iota((depth, 1), 0)
    by_band = (row // r == iota((depth, n_bands), 1)).astype(BF16)
    v_rows = jnp.dot(by_band, vl.astype(BF16), preferred_element_type=F32)
    for s in range(n_src):
        by_src = (row % r + s * r == iota((depth, n_src * r), 1)).astype(BF16)
        p_rows = jnp.dot(by_src, ph.astype(BF16), preferred_element_type=F32)
        w_ref[s * depth : (s + 1) * depth, :] = (p_rows * v_rows).astype(BF16)


def group_sums(coupled, kg, gauss_ref, occ_ref, n_bands, ph):
    per = 128 // n_bands
    n_vg = coupled.shape[1] // 128
    sums = []
    for k in range(per):
        here = slice(k * n_bands, (k + 1) * n_bands)
        rows = slice(kg * 128 + k * n_bands, kg * 128 + (k + 1) * n_bands)
        occ = occ_ref[0, rows, :]
        el = None
        for vg in range(n_vg):
            c = coupled[here, vg * 128 : (vg + 1) * 128]
            strength = c * c * gauss_ref[0, rows, vg * 128 : (vg + 1) * 128].astype(F32)
            el = strength if el is None else el + strength
            weighed = strength * occ
            weighed = sum(weighed[x : x + 8] for x in range(0, n_bands, 8))
            ph[k][vg] = weighed if ph[k][vg] is None else ph[k][vg] + weighed
        sums.append(el)
    sums.append(jnp.zeros((128 - per * n_bands, 128), F32))
    return jnp.sum(jnp.concatenate(sums, axis=0).T, axis=0, keepdims=True)


def product_and_sums(a_ref, w_ref, t_new, t_old, bd_ref, gauss_ref, occ_ref, ph_scr, scale, n_bands, n_v, fill):
    per = 128 // n_bands
    n_vg = -(-n_v // per)
    ph = [[None] * n_vg for _ in range(per)]
    t_new[...] = jnp.dot(a_ref[...], w_ref[...], preferred_element_type=F32)
    fill()
    right = swap_blocks(t_old, 0, n_bands, n_v)
    c0 = jnp.dot(bd_ref[0, 0], right, preferred_element_type=F32)
    right = swap_blocks(t_old, 1, n_bands, n_v)
    el0 = group_sums(c0, 0, gauss_ref, occ_ref, n_bands, ph)
    c1 = jnp.dot(bd_ref[0, 1], right, preferred_element_type=F32)
    el1 = group_sums(c1, 1, gauss_ref, occ_ref, n_bands, ph)
    for k in range(per):
        for vg in range(n_vg):
            add = ph[k][vg] if scale is None else ph[k][vg] * scale
            ph_scr[k, :, vg * 128 : (vg + 1) * 128] += add
    return [el0, el1]


def linewidth_kernel(n_bands, n_v, halves, r, tiles, k_dev, el_scale, ph_scale, a_ref, *refs):
    refs = list(refs)
    take = lambda n: [refs.pop(0) for _ in range(n)]
    unroll = UNROLL
    sources = take(4)
    (send_out,) = take(1)
    held, (sems,) = take(4), take(1)
    pv_ref, bd_ref, gauss_ref, occ_ref = held
    (a_scr,), w_scr, t_scr, (ph_scr,), (el_scr,) = take(1), take(unroll), take(unroll), take(1), take(1)
    g = pl.program_id(0)
    last = pl.num_programs(0) - 1
    steps = -(-(tiles + 1) // unroll)
    per = 128 // n_bands
    n_src, rows, wide = a_ref.shape
    depth = wide // halves
    n_vg = ph_scr.shape[2] // 128

    def copy(which, step):
        part = pl.ds(step * unroll, unroll)
        return pltpu.make_async_copy(sources[which].at[part], held[which].at[part], sems.at[which, step])

    @pl.when(g == 0)
    def _():
        for which in range(4):
            copy(which, 0).start()
        for step in range(1, steps):
            for which in range(4):
                copy(which, step).start()
        for s in range(n_src):
            block = a_ref[s]
            for h in range(halves):
                a_scr[h * rows : (h + 1) * rows, s * depth : (s + 1) * depth] = block[
                    :, h * depth : (h + 1) * depth
                ]
        t_scr[-1][...] = jnp.zeros_like(t_scr[-1])
        ph_scr[...] = jnp.zeros_like(ph_scr)
        copy(0, 0).wait()
        fill_products(w_scr[0], pv_ref[0], n_bands, r)

    @pl.when(g < last)
    def _():
        copy(0, g + 1).wait()

    for which in range(1, 4):
        copy(which, g).wait()

    def tile_of(ref, n):
        return ref.at[pl.ds(jnp.clip(unroll * g + n, 0, tiles - 1), 1)]

    el = []
    for x in range(unroll):
        beyond = (steps - 1) * unroll + x - 1 >= tiles
        scale = jnp.where(g < last, 1.0, 0.0) if beyond else None
        el += product_and_sums(
            a_scr, w_scr[x], t_scr[x], t_scr[x - 1], tile_of(bd_ref, x - 1), tile_of(gauss_ref, x - 1), tile_of(occ_ref, x - 1),
            ph_scr, scale, n_bands, n_v,
            lambda: fill_products(w_scr[(x + 1) % unroll], tile_of(pv_ref, x + 1)[0], n_bands, r),
        )
    el_scr[pl.ds(g * 8, 8), :] = jnp.concatenate(el + [jnp.zeros((8 - 2 * unroll, 128), F32)], axis=0)

    @pl.when(g == last)
    def _():
        fold = (iota((128, 128), 0) // n_bands == iota((128, 128), 1)).astype(F32)
        rows = []
        for vg in range(n_vg):
            row = jnp.zeros((8, 128), F32)
            for k in range(per):
                tile = ph_scr[k, :, vg * 128 : (vg + 1) * 128]
                row = row + (pltpu.roll(tile, 128 - n_bands * k, 1) if k else tile)
            rows.append(jnp.sum(row, axis=0, keepdims=True))
        sums = jnp.dot(
            jnp.concatenate(rows, axis=0), fold,
            precision=lax.Precision.HIGHEST, preferred_element_type=F32,
        )
        used = per * n_bands
        n_ka, n_pb, n_row, n_rows, _ = send_out.shape
        sums = pltpu.roll(sums * ph_scale, used, 1)
        sums = jnp.concatenate([sums, jnp.zeros((n_rows - n_vg, 128), F32)], axis=0)
        groups = [el_scr[g_ * 8 : g_ * 8 + 2 * unroll, :] for g_ in range(steps)]
        groups = jnp.concatenate(groups + [jnp.zeros((n_rows, 128), F32)], axis=0) * el_scale
        lane = iota((n_rows, 128), 1)
        for d in range(n_ka * n_row):
            lo = 2 + d * k_dev // per
            part = jnp.where(lane < used, groups[lo : lo + n_rows], sums)
            for pb in range(n_pb):
                send_out[d // n_row, pb, d % n_row] = part


def linewidths(a, prepared, k_loc, k_dev, n_row, n_pb, n_bands, n_v, halves, r, el_scale, ph_scale):
    pv, bd, gauss, occ = prepared
    per = 128 // n_bands
    unroll = UNROLL
    tiles, steps = steps_of(k_loc, n_bands)
    n_vg = gauss.shape[2] // 128
    total = (pv.shape[1] - n_bands) * n_bands

    a = pltpu.with_memory_space_constraint(a, pltpu.VMEM)
    tables = [pltpu.with_memory_space_constraint(x, pltpu.HBM) for x in (pv, bd, gauss, occ)]
    n_rows = -(-(-(-(per - 1 + k_dev) // per)) // 8) * 8
    n_ka = k_loc // k_dev // n_row
    return pl.pallas_call(
        functools.partial(
            linewidth_kernel, n_bands, n_v, halves, r, tiles, k_dev, el_scale, ph_scale
        ),
        grid=(steps,),
        in_specs=[pl.BlockSpec(memory_space=pltpu.VMEM)]
        + [pl.BlockSpec(memory_space=pltpu.HBM)] * len(tables),
        out_specs=pl.BlockSpec((n_ka, n_pb, n_row, n_rows, 128), lambda g: (0,) * 5),
        out_shape=jax.ShapeDtypeStruct((n_ka, n_pb, n_row, n_rows, 128), F32),
        scratch_shapes=[pltpu.VMEM(x.shape, x.dtype) for x in tables]
        + [pltpu.SemaphoreType.DMA((len(tables), steps))]
        + [pltpu.VMEM((n_v * n_bands, total), BF16)]
        + [pltpu.VMEM((total, 256), BF16)] * unroll
        + [pltpu.VMEM((n_v * n_bands, 256), F32)] * unroll
        + [pltpu.VMEM((per, 8, n_vg * 128), F32), pltpu.VMEM((steps * 8, 128), F32)],
        compiler_params=VMEM,
        name="linewidths",
    )(a, *tables)


def on_device(coupling, rotation, freq, eigvec, energies, window, kq_index, kpoints, lattice):
    plane = ("ka", "row")
    everywhere = ("ka", "pb", "row")
    n_ka = lax.axis_size("ka")
    n_row = lax.axis_size("row")
    n_pb = lax.axis_size("pb")
    n_group = n_ka * n_row
    k_dev, n_bands = eigvec.shape[:2]
    q_dev, n_modes = rotation.shape[:2]
    assert q_dev == n_row
    pair = n_bands * n_bands
    total_k = k_dev * n_group
    total_q = q_dev * n_pb
    v_parts = math.gcd(n_modes, n_ka)
    k_parts = n_ka // v_parts
    n_v = n_modes // v_parts
    halves = 2 if n_v % 2 == 0 else 1
    k_loc = total_k // k_parts
    ka_pos = lax.axis_index("ka")
    row_pos = lax.axis_index("row")
    pb_pos = lax.axis_index("pb")

    points = pack(eigvec, energies, window, n_group)
    points = lax.all_to_all(points, plane, 0, 0, tiled=True).reshape(total_k, -1)

    pad = -coupling.shape[1] % 8
    if pad:
        coupling = jnp.pad(coupling, ((0, 0), (0, pad), (0, 0)))
    r, r_sent = coupling.shape[1] - pad, coupling.shape[1]
    rotated = rotate(coupling, rotation, n_bands, v_parts, halves)
    if k_parts > 1:
        rotated = jnp.repeat(rotated, k_parts, axis=0)
    rotated = rotated.reshape((n_group,) + rotated.shape[2:])
    a = lax.all_to_all(rotated, plane, 0, 0, tiled=True)
    if pad:
        a = a.reshape(a.shape[:2] + (halves * n_bands, r_sent))[..., :r]
        a = a.reshape(a.shape[:2] + (halves * n_bands * r,))

    k_start = (ka_pos % k_parts) * k_loc
    kp = lax.dynamic_slice_in_dim(kpoints, k_start, k_loc, 0)
    phase = phase_table(lattice, kp)
    kq = lax.dynamic_slice(kq_index, (row_pos, k_start), (1, k_loc))
    v_start = (ka_pos // k_parts) * n_v
    freq_mine = lax.dynamic_slice(freq, (row_pos, v_start), (1, n_v))
    points = pltpu.with_memory_space_constraint(points, pltpu.VMEM)
    prepared = prepare(
        freq_mine, k_start[None], kq, points, phase, n_bands, n_v
    )
    norm = 1.0 / (math.sqrt(2.0 * math.pi) * SIGMA)
    send = linewidths(
        a, prepared, k_loc, k_dev, n_row, n_pb, n_bands, n_v, halves, r,
        norm / (total_q * n_modes * n_bands), norm / (total_k * n_bands),
    )
    if k_parts > 1:
        used = 128 // n_bands * n_bands
        rest = jnp.where(jnp.arange(128) < used, 0.0, send[:1])
        rest = jnp.broadcast_to(rest, (n_ka,) + send.shape[1:])
        send = lax.dynamic_update_slice_in_dim(rest, send, k_start // (k_dev * n_row), 0)
    got = lax.all_to_all(
        send.reshape((n_group * n_pb,) + send.shape[3:]), everywhere, 0, 0, tiled=True
    ).reshape(send.shape)
    n_local = k_loc // k_dev
    first = (ka_pos * n_row + row_pos) % n_local * k_dev % (128 // n_bands)
    place = jnp.stack([pb_pos, first]).astype(jnp.int32)
    electron, phonon = finish(got, place, n_bands, n_v, k_parts, k_dev, n_modes)
    return (electron, phonon)


def solution(mesh):
    return jax.shard_map(
        on_device,
        mesh=mesh,
        in_specs=(
            P("pb", ("ka", "row"), None),
            P("pb", None, None),
            P("pb", None),
            P(("ka", "row"), None, None),
            P(("ka", "row"), None),
            P(("ka", "row")),
            P("pb", None),
            P(),
            P(),
        ),
        out_specs=(P(("ka", "row"), None), P("pb", None)),
        check_vma=False,
    )
```

```python
import functools
import math

import jax
import jax.numpy as jnp
import numpy as np
from jax import lax
from jax.experimental import pallas as pl
from jax.experimental.pallas import tpu as pltpu
from jax.sharding import PartitionSpec as P

SIGMA = 0.1
THERMAL_ENERGY_KT = 0.2
VMEM = pltpu.CompilerParams(vmem_limit_bytes=40 * 1024 * 1024)
F32 = jnp.float32
BF16 = jnp.bfloat16
UNROLL = 3
K_PER = 4


def phase_rows(lattice, kpoint_rows):
    rvec = lattice.astype(jnp.float32)
    argument = (
        rvec[:, 0][None, :] * kpoint_rows[:, 0:1]
        + rvec[:, 1][None, :] * kpoint_rows[:, 1:2]
        + rvec[:, 2][None, :] * kpoint_rows[:, 2:3]
    )
    return jnp.cos(2.0 * math.pi * argument).astype(jnp.bfloat16)


def iota(shape, dim):
    return lax.broadcasted_iota(jnp.int32, shape, dim)


def pack_kernel(eig_ref, en_ref, window_ref, out_ref):
    n_bands, _, k_dev = eig_ref.shape
    rest = en_ref[...]
    high = rest.astype(BF16).astype(F32)
    rows = [eig_ref[...].astype(F32).reshape(n_bands * n_bands, k_dev), high, rest - high]
    rows.append(window_ref[...].astype(F32))
    rows.append(jnp.zeros((out_ref.shape[2] - n_bands * (n_bands + 2) - 1, k_dev), F32))
    packed = jnp.concatenate(rows, axis=0)
    packed = jnp.concatenate([packed, jnp.zeros((packed.shape[0], 128 - k_dev), F32)], axis=1)
    packed = packed.T[:k_dev].astype(BF16)
    for d in range(out_ref.shape[0]):
        out_ref[d] = packed


def pack(eigvec, energies, window, copies):
    k_dev, n_bands, _ = eigvec.shape
    wide = -(-(n_bands * (n_bands + 2) + 1) // 128) * 128
    args = (eigvec.transpose(1, 2, 0), energies.T, window.reshape(1, k_dev))
    return pl.pallas_call(
        pack_kernel,
        grid=(1,),
        in_specs=[pl.BlockSpec(x.shape, lambda g, n=x.ndim: (0,) * n) for x in args],
        out_specs=pl.BlockSpec(memory_space=pltpu.VMEM),
        out_shape=pltpu.VMEM((copies, k_dev, wide), BF16),
        compiler_params=VMEM,
        name="pack_points",
    )(*[pltpu.with_memory_space_constraint(x, pltpu.HBM) for x in args])


def finish_kernel(n_bands, n_v, k_parts, place_ref, got_ref, el_out, ph_out, scr):
    n_ka, n_pb, n_row, rows, _ = got_ref.shape
    lane = iota((1, 128), 1)
    total = None
    for ka in range(n_ka):
        for pb in range(n_pb):
            for row in range(n_row):
                part = got_ref[ka, pb, row]
                total = part if total is None else total + part
    for x in range(K_PER):
        scr[pl.ds(x, rows, stride=K_PER), :] = pltpu.roll(total, 128 - n_bands * x, 1) if x else total
    k_dev = el_out.shape[1]
    mine = jnp.concatenate([scr[...], jnp.zeros((128 - k_dev, 128), F32)], axis=0)
    el_out[...] = mine.T[:n_bands, :k_dev]
    for row in range(n_row):
        line = jnp.zeros((1, 128), F32)
        for ka in range(n_ka):
            part = got_ref[ka, pl.ds(place_ref[0], 1), row][0]
            to = ka // k_parts * n_v
            moved = pltpu.roll(part[0:1], (to - K_PER * n_bands) % 128, 1)
            line = line + jnp.where((lane >= to) & (lane < to + n_v), moved, 0.0)
        ph_out[row : row + 1, :] = line[:, : ph_out.shape[1]]


def finish(got, place, n_bands, n_v, k_parts, k_dev, n_modes):
    n_row, rows = got.shape[2:4]
    el, ph = pl.pallas_call(
        functools.partial(finish_kernel, n_bands, n_v, k_parts),
        in_specs=[pl.BlockSpec(memory_space=pltpu.SMEM), pl.BlockSpec(memory_space=pltpu.VMEM)],
        out_shape=[
            jax.ShapeDtypeStruct((n_bands, k_dev), F32),
            jax.ShapeDtypeStruct((n_row, n_modes), F32),
        ],
        scratch_shapes=[pltpu.VMEM((rows * K_PER, 128), F32)],
        compiler_params=VMEM,
        name="finish",
    )(place, pltpu.with_memory_space_constraint(got, pltpu.VMEM))
    return el.T, ph


def rotate_kernel(n_modes, n_bands, v_parts, coup_ref, rot_ref, out_ref):
    r = coup_ref.shape[1]
    pair = n_bands * n_bands
    rows = n_modes * r
    x = coup_ref[0].astype(F32)
    x = jnp.concatenate([x[:, c * pair : (c + 1) * pair] for c in range(n_modes)], axis=0).astype(BF16)
    rot = rot_ref[...].astype(F32)
    rot = jnp.sum(jnp.where(iota(rot.shape, 1) == pl.program_id(0), rot, 0.0), axis=1).astype(BF16)
    spread_v = (iota((rows, n_modes), 0) // r == iota((rows, n_modes), 1)).astype(BF16)
    spread_c = (iota((n_modes, rows), 1) // r == iota((n_modes, rows), 0)).astype(BF16)
    half = lax.dot_general(spread_v, rot, (((1,), (1,)), ((), ())), preferred_element_type=F32)
    full = jnp.dot(half.astype(BF16), spread_c, preferred_element_type=F32)
    same = iota((rows, rows), 0) % r == iota((rows, rows), 1) % r
    big = jnp.where(same, full, 0.0).astype(BF16)
    y = jnp.dot(big, x, preferred_element_type=F32)
    n_v = n_modes // v_parts
    half_i = n_bands // 2
    wide = out_ref.shape[3]
    for part in range(v_parts):
        pieces = []
        for i in range(half_i):
            block = [
                y[v * r : (v + 1) * r, x * n_bands : (x + 1) * n_bands]
                for x in (i, i + half_i)
                for v in range(part * n_v, (part + 1) * n_v)
            ]
            if wide > 2 * n_v * n_bands:
                block.append(jnp.zeros((r, wide - 2 * n_v * n_bands), F32))
            pieces.append(jnp.concatenate(block, axis=1))
        out_ref[part, 0] = jnp.concatenate(pieces, axis=0).astype(BF16)


def rotate(coupling, rotation, n_bands, v_parts):
    q, r, width = coupling.shape
    n_modes = rotation.shape[1]
    rows = n_bands // 2 * r
    cols = -(-(2 * n_modes // v_parts * n_bands) // 128) * 128
    return pl.pallas_call(
        functools.partial(rotate_kernel, n_modes, n_bands, v_parts),
        grid=(q,),
        in_specs=[
            pl.BlockSpec((1, r, width), lambda a: (a, 0, 0)),
            pl.BlockSpec((n_modes, q, n_modes), lambda a: (0, 0, 0)),
        ],
        out_specs=pl.BlockSpec((v_parts, 1, rows, cols), lambda a: (0, a, 0, 0)),
        out_shape=jax.ShapeDtypeStruct((v_parts, q, rows, cols), BF16),
        compiler_params=VMEM,
        name="rotate_modes",
    )(
        pltpu.with_memory_space_constraint(coupling, pltpu.HBM),
        pltpu.with_memory_space_constraint(rotation.transpose(1, 0, 2), pltpu.HBM),
    )


def steps_of(k_loc):
    tiles = k_loc // (2 * K_PER)
    return tiles, -(-(tiles + 1) // UNROLL)


def prepare_kernel(
    n_bands, n_v, k_loc,
    freq_ref, start_ref, kq_ref, points_ref,
    wt_out, bd_out, gauss_out, occ_out,
    eig_scr, en_scr, keep_scr,
):
    g = pl.program_id(0)
    used = K_PER * n_bands
    k_all = points_ref.shape[0]
    at_en = points_ref.shape[1] - 128
    slots = 2 * K_PER
    scale = 1.0 / (SIGMA * math.sqrt(2.0))
    lane = iota((1, 128), 1)
    roll = lambda x, shift: pltpu.roll(x, shift % 128, 1) if shift % 128 else x

    @pl.when(g == 0)
    def _():
        en = roll(points_ref[:, at_en:].astype(F32), -(n_bands * n_bands % 128))
        lim = en[:, 2 * n_bands : 2 * n_bands + 1]
        en_scr[...] = jnp.where(lane < n_bands, en + roll(en, -n_bands), 0.0)
        keep = lane.astype(F32) < jnp.minimum(lim, float(n_bands))
        for i in range(n_bands):
            lo = i * n_bands
            tile = lo // 128 * 128
            block = roll(points_ref[:, tile : tile + 128].astype(F32), tile - lo)
            if lo + n_bands > tile + 128:
                more = roll(points_ref[:, tile + 128 : tile + 256].astype(F32), tile - lo)
                block = jnp.where(lane < tile + 128 - lo, block, more)
            eig_scr[pl.ds(i, k_all, stride=n_bands), :] = jnp.where(keep, block, 0.0)
        shape = (slots * n_bands, slots * n_bands)
        keep_scr[...] = (iota(shape, 0) // n_bands == iota(shape, 1) % slots).astype(BF16)

    by_band = (iota((n_bands, slots * n_bands), 0) == iota((n_bands, slots * n_bands), 1) // slots).astype(BF16)
    for step in range(UNROLL):
        t = g * UNROLL + step
        first = jnp.minimum(t * slots, k_loc - slots)
        v_tiles = []
        blocks = []
        for kg in range(2):
            vl = None
            level = None
            diagonal = []
            far_rows = []
            for x in range(K_PER):
                k = first + kg * K_PER + x
                near = k + start_ref[0]
                far = kq_ref[0, k]
                v = roll(eig_scr[pl.ds(pl.multiple_of(far * n_bands, 8), n_bands), :], n_bands * x)
                u = roll(eig_scr[pl.ds(pl.multiple_of(near * n_bands, 8), n_bands), :], n_bands * x)
                e = roll(en_scr[pl.ds(near, 1), :], n_bands * x)
                vl = v if vl is None else vl + v
                level = e if level is None else level + e
                diagonal.append(u)
                far_rows.append(jnp.broadcast_to(en_scr[pl.ds(far, 1), :], (n_bands, 128)))
            v_tiles.append(vl)
            blocks.append(jnp.concatenate(diagonal + [jnp.zeros((128 - used, 128), F32)], axis=0))
            cols = slice(kg * 128, (kg + 1) * 128)
            far_e = jnp.concatenate(far_rows + [jnp.zeros((128 - used, 128), F32)], axis=0).T[:n_bands]
            occ_out[step, :, cols] = jax.nn.sigmoid(-level / THERMAL_ENERGY_KT) - jax.nn.sigmoid(
                -far_e / THERMAL_ENERGY_KT
            )
            base = (far_e - level) * scale
            for v in range(0, n_v, 2):
                both = []
                for x in range(v, min(v + 2, n_v)):
                    d = base - freq_ref[0, x] * scale
                    both.append(jnp.exp(-(d * d)))
                rows = slice(v * n_bands, (v + len(both)) * n_bands)
                gauss_out[step, rows, cols] = jnp.concatenate(both, axis=0).astype(BF16)
        zero = jnp.zeros((128, 128), F32)
        bd_out[step, :128, :] = jnp.concatenate([blocks[0], zero], axis=1).astype(BF16)
        bd_out[step, 128:, :] = jnp.concatenate([zero, blocks[1]], axis=1).astype(BF16)
        vl = jnp.concatenate(v_tiles, axis=1).astype(BF16)
        wt = lax.dot_general(vl, by_band, (((0,), (0,)), ((), ())), preferred_element_type=F32)
        wt = jnp.concatenate([wt[:used], wt[128 : 128 + used]], axis=0)
        wt_out[step] = wt.astype(BF16) * keep_scr[...]


def prepare(freq, start, kq, points, n_bands, n_v):
    k_loc = kq.shape[1]
    steps = steps_of(k_loc)[1]
    tiles = steps * UNROLL
    k_all = points.shape[0]
    wide = 2 * K_PER * n_bands
    smem = pl.BlockSpec(memory_space=pltpu.SMEM)
    shapes = ((wide, wide), (256, 256), (n_v * n_bands, 256), (n_bands, 256))
    types = (BF16, BF16, BF16, F32)
    return pl.pallas_call(
        functools.partial(prepare_kernel, n_bands, n_v, k_loc),
        grid=(steps,),
        in_specs=[smem, smem, smem, pl.BlockSpec(memory_space=pltpu.VMEM)],
        out_specs=[pl.BlockSpec((UNROLL,) + x, lambda g: (g, 0, 0)) for x in shapes],
        out_shape=[pltpu.HBM((tiles,) + x, t) for x, t in zip(shapes, types)],
        scratch_shapes=[
            pltpu.VMEM((k_all * n_bands, 128), F32),
            pltpu.VMEM((k_all, 128), F32),
            pltpu.VMEM((wide, wide), BF16),
        ],
        compiler_params=VMEM,
        name="prepare",
    )(freq, start, kq, points)


def swap_blocks(t_ref, n_bands, n_v):
    v_per = 128 // n_bands
    lane = iota((n_bands, 128), 1)
    inside = []
    for d in range(v_per + K_PER - 1):
        lo = n_bands * d % 128
        hi = lo + n_bands
        inside.append(
            (lane >= lo) & (lane < hi) if hi <= 128 else (lane >= lo) | (lane < hi - 128)
        )
    halves = []
    for kg in range(2):
        column = []
        for first in range(0, n_v, v_per):
            vg = first // v_per
            rolled = []
            for k in range(K_PER):
                row = (kg * K_PER + k) * n_bands
                block = t_ref[row : row + n_bands, vg * 128 : (vg + 1) * 128]
                rolled.append(pltpu.roll(block, n_bands * k, 1) if k else block)
            for v in range(min(v_per, n_v - first)):
                mix = rolled[0]
                for k in range(1, K_PER):
                    mix = jnp.where(inside[v + k], rolled[k], mix)
                column.append(pltpu.roll(mix, 128 - n_bands * v, 1) if v else mix)
        halves.append(jnp.concatenate(column, axis=0).astype(BF16))
    return jnp.concatenate(halves, axis=1)


def tile_step(wt_ref, b_ref, t_new, t_old, bd_ref, gauss_ref, occ_ref, ph_scr, scale, n_bands, n_v):
    t_new[...] = jnp.dot(wt_ref[0], b_ref[0], preferred_element_type=F32)
    left = swap_blocks(t_old, n_bands, n_v)
    coupled = jnp.dot(left, bd_ref[0], preferred_element_type=F32)
    occ = occ_ref[0]
    el = None
    for v in range(0, n_v, 2):
        count = min(2, n_v - v)
        gauss = gauss_ref[0, v * n_bands : (v + count) * n_bands, :].astype(F32)
        for x in range(count):
            c = coupled[(v + x) * n_bands : (v + x + 1) * n_bands]
            strength = c * c * gauss[x * n_bands : (x + 1) * n_bands]
            el = strength if el is None else el + strength
            weighed = strength * occ
            weighed = sum(weighed[z : z + 8] for z in range(0, n_bands, 8))
            weighed = weighed[:, :128] + weighed[:, 128:]
            ph_scr[v + x] += weighed if scale is None else weighed * scale
    el = jnp.sum(el, axis=0, keepdims=True)
    return [el[:, :128], el[:, 128:]]


def linewidth_kernel(n_bands, n_v, r, tiles, k_dev, el_scale, ph_scale, a_ref, phase_ref, *refs):
    refs = list(refs)
    take = lambda n: [refs.pop(0) for _ in range(n)]
    unroll = UNROLL
    sources = take(4)
    (send_out,) = take(1)
    held, (sems,) = take(4), take(1)
    wt_ref, bd_ref, gauss_ref, occ_ref = held
    (a_scr, b_scr, ph_scr, el_scr), t_scr = take(4), take(unroll)
    g = pl.program_id(0)
    last = pl.num_programs(0) - 1
    steps = -(-(tiles + 1) // unroll)
    n_src = a_ref.shape[0]
    half_i = n_bands // 2
    v_per = 128 // n_bands
    cols = n_v * n_bands
    slots = 2 * K_PER

    def copy(which, step):
        part = pl.ds(step * unroll, unroll)
        return pltpu.make_async_copy(sources[which].at[part], held[which].at[part], sems.at[which, step])

    @pl.when(g == 0)
    def _():
        for step in range(steps):
            for which in range(4):
                copy(which, step).start()
        lane = iota((1, 128), 1)
        for s in range(0, n_src, 2):
            for h in range(2):
                for vg in range(-(-n_v // v_per)):
                    lo = h * cols + vg * v_per * n_bands
                    tile, off = lo // 128 * 128, lo % 128
                    both = []
                    for x in (s, s + 1):
                        block = a_ref[x, :, tile : tile + 128].astype(F32)
                        if off:
                            block = pltpu.roll(block, 128 - off, 1)
                            if tile + 128 < a_ref.shape[2]:
                                more = a_ref[x, :, tile + 128 : tile + 256].astype(F32)
                                block = jnp.where(lane < 128 - off, block, pltpu.roll(more, 128 - off, 1))
                        both.append(block)
                    for i in range(half_i):
                        here = slice(i * r, (i + 1) * r)
                        a_scr[h * half_i + i, s * r : (s + 2) * r, vg * 128 : (vg + 1) * 128] = (
                            jnp.concatenate([both[0][here], both[1][here]], axis=0).astype(BF16)
                        )
        for i in range(0, n_bands, 2):
            b0 = jnp.dot(phase_ref[...], a_scr[i], preferred_element_type=F32)
            b1 = jnp.dot(phase_ref[...], a_scr[i + 1], preferred_element_type=F32)
            for t in range(tiles):
                here = slice(t * slots, (t + 1) * slots)
                b_scr[t, i * slots : (i + 2) * slots, :] = jnp.concatenate(
                    [b0[here], b1[here]], axis=0
                ).astype(BF16)
        t_scr[-1][...] = jnp.zeros_like(t_scr[-1])
        ph_scr[...] = jnp.zeros_like(ph_scr)

    for which in range(4):
        copy(which, g).wait()

    def tile_of(ref, n):
        return ref.at[pl.ds(jnp.clip(unroll * g + n, 0, tiles - 1), 1)]

    el = []
    for x in range(unroll):
        beyond = (steps - 1) * unroll + x - 1 >= tiles
        scale = jnp.where(g < last, 1.0, 0.0) if beyond else None
        el += tile_step(
            tile_of(wt_ref, x), tile_of(b_scr, x), t_scr[x], t_scr[x - 1], tile_of(bd_ref, x - 1),
            tile_of(gauss_ref, x - 1), tile_of(occ_ref, x - 1), ph_scr, scale, n_bands, n_v,
        )
    el_scr[pl.ds(g * 8, 8), :] = jnp.concatenate(el + [jnp.zeros((8 - 2 * unroll, 128), F32)], axis=0)

    @pl.when(g == last)
    def _():
        used = K_PER * n_bands
        n_ka, n_pb, n_row, n_rows, _ = send_out.shape
        sums = jnp.sum(ph_scr[...], axis=1)
        sums = jnp.concatenate([sums, jnp.zeros((128 - n_v, 128), F32)], axis=0).T
        sums = pltpu.roll(jnp.sum(sums, axis=0, keepdims=True) * ph_scale, used, 1)
        groups = [el_scr[x * 8 : x * 8 + 2 * unroll, :] for x in range(steps)]
        groups = jnp.concatenate(groups, axis=0) * el_scale
        lane = iota((n_rows, 128), 1)
        for d in range(n_ka * n_row):
            lo = 2 + d * n_rows
            part = jnp.where(lane < used, groups[lo : lo + n_rows], sums)
            for pb in range(n_pb):
                send_out[d // n_row, pb, d % n_row] = part


def linewidths(a, phase, prepared, k_loc, k_dev, n_row, n_pb, n_bands, n_v, r, el_scale, ph_scale):
    wt, bd, gauss, occ = prepared
    tiles, steps = steps_of(k_loc)
    lanes = -(-n_v // (128 // n_bands)) * 128
    wide = 2 * K_PER * n_bands
    depth = a.shape[0] * r
    a = pltpu.with_memory_space_constraint(a, pltpu.VMEM)
    tables = [pltpu.with_memory_space_constraint(x, pltpu.HBM) for x in (wt, bd, gauss, occ)]
    n_rows = k_dev // K_PER
    n_ka = k_loc // k_dev // n_row
    return pl.pallas_call(
        functools.partial(linewidth_kernel, n_bands, n_v, r, tiles, k_dev, el_scale, ph_scale),
        grid=(steps,),
        in_specs=[pl.BlockSpec(memory_space=pltpu.VMEM)] * 2
        + [pl.BlockSpec(memory_space=pltpu.HBM)] * len(tables),
        out_specs=pl.BlockSpec((n_ka, n_pb, n_row, n_rows, 128), lambda g: (0,) * 5),
        out_shape=jax.ShapeDtypeStruct((n_ka, n_pb, n_row, n_rows, 128), F32),
        scratch_shapes=[pltpu.VMEM(x.shape, x.dtype) for x in tables]
        + [pltpu.SemaphoreType.DMA((len(tables), steps))]
        + [
            pltpu.VMEM((n_bands, depth, lanes), BF16),
            pltpu.VMEM((tiles, wide, lanes), BF16),
            pltpu.VMEM((n_v, 8, 128), F32),
            pltpu.VMEM((steps * 8, 128), F32),
        ]
        + [pltpu.VMEM((wide, lanes), F32)] * UNROLL,
        compiler_params=VMEM,
        name="linewidths",
    )(a, phase, *tables)


def on_device(coupling, rotation, freq, eigvec, energies, window, kq_index, kpoints, lattice):
    plane = ("ka", "row")
    everywhere = ("ka", "pb", "row")
    n_ka = lax.axis_size("ka")
    n_row = lax.axis_size("row")
    n_pb = lax.axis_size("pb")
    n_group = n_ka * n_row
    k_dev, n_bands = eigvec.shape[:2]
    q_dev, n_modes = rotation.shape[:2]
    assert q_dev == n_row
    pair = n_bands * n_bands
    total_k = k_dev * n_group
    total_q = q_dev * n_pb
    v_parts = math.gcd(n_modes, n_ka)
    k_parts = n_ka // v_parts
    n_v = n_modes // v_parts
    k_loc = total_k // k_parts
    ka_pos = lax.axis_index("ka")
    row_pos = lax.axis_index("row")
    pb_pos = lax.axis_index("pb")

    points = pack(eigvec, energies, window, n_group)
    points = lax.all_to_all(points, plane, 0, 0, tiled=True).reshape(total_k, -1)

    pad = -coupling.shape[1] % 8
    if pad:
        coupling = jnp.pad(coupling, ((0, 0), (0, pad), (0, 0)))
    r = coupling.shape[1]
    rotated = rotate(coupling, rotation, n_bands, v_parts)
    if k_parts > 1:
        rotated = jnp.repeat(rotated, k_parts, axis=0)
    rotated = rotated.reshape((n_group,) + rotated.shape[2:])
    a = lax.all_to_all(rotated, plane, 0, 0, tiled=True)
    k_start = (ka_pos % k_parts) * k_loc
    kp = lax.dynamic_slice_in_dim(kpoints, k_start, k_loc, 0)
    phase = phase_rows(lattice, kp)
    if pad:
        phase = jnp.pad(phase.reshape(k_loc, n_group, r - pad), ((0, 0), (0, 0), (0, pad)))
        phase = phase.reshape(k_loc, n_group * r)
    kq = lax.dynamic_slice(kq_index, (row_pos, k_start), (1, k_loc))
    v_start = (ka_pos // k_parts) * n_v
    freq_mine = lax.dynamic_slice(freq, (row_pos, v_start), (1, n_v))
    points = pltpu.with_memory_space_constraint(points, pltpu.VMEM)
    prepared = prepare(freq_mine, k_start[None], kq, points, n_bands, n_v)
    norm = 1.0 / (math.sqrt(2.0 * math.pi) * SIGMA)
    send = linewidths(
        a, phase, prepared, k_loc, k_dev, n_row, n_pb, n_bands, n_v, r,
        norm / (total_q * n_modes * n_bands), norm / (total_k * n_bands),
    )
    if k_parts > 1:
        used = K_PER * n_bands
        rest = jnp.where(jnp.arange(128) < used, 0.0, send[:1])
        rest = jnp.broadcast_to(rest, (n_ka,) + send.shape[1:])
        send = lax.dynamic_update_slice_in_dim(rest, send, k_start // (k_dev * n_row), 0)
    got = lax.all_to_all(
        send.reshape((n_group * n_pb,) + send.shape[3:]), everywhere, 0, 0, tiled=True
    ).reshape(send.shape)
    place = pb_pos[None].astype(jnp.int32)
    electron, phonon = finish(got, place, n_bands, n_v, k_parts, k_dev, n_modes)
    return (electron, phonon)


def solution(mesh):
    return jax.shard_map(
        on_device,
        mesh=mesh,
        in_specs=(
            P("pb", ("ka", "row"), None),
            P("pb", None, None),
            P("pb", None),
            P(("ka", "row"), None, None),
            P(("ka", "row"), None),
            P(("ka", "row")),
            P("pb", None),
            P(),
            P(),
        ),
        out_specs=(P(("ka", "row"), None), P("pb", None)),
        check_vma=False,
    )
```

```python
import functools
import math

import jax
import jax.numpy as jnp
import numpy as np
from jax import lax
from jax.experimental import pallas as pl
from jax.experimental.pallas import tpu as pltpu
from jax.sharding import PartitionSpec as P

SIGMA = 0.1
THERMAL_ENERGY_KT = 0.2
VMEM = pltpu.CompilerParams(vmem_limit_bytes=40 * 1024 * 1024)
F32 = jnp.float32
BF16 = jnp.bfloat16
UNROLL = 11
PREPARED = 3
K_PER = 4


def phase_rows(lattice, kpoint_rows):
    rvec = lattice.astype(jnp.float32)
    argument = (
        rvec[:, 0][None, :] * kpoint_rows[:, 0:1]
        + rvec[:, 1][None, :] * kpoint_rows[:, 1:2]
        + rvec[:, 2][None, :] * kpoint_rows[:, 2:3]
    )
    return jnp.cos(2.0 * math.pi * argument).astype(jnp.bfloat16)


def iota(shape, dim):
    return lax.broadcasted_iota(jnp.int32, shape, dim)


def pack_kernel(eig_ref, en_ref, window_ref, out_ref):
    n_bands, _, k_dev = eig_ref.shape
    rest = en_ref[...]
    high = rest.astype(BF16).astype(F32)
    rows = [eig_ref[...].astype(F32).reshape(n_bands * n_bands, k_dev), high, rest - high]
    rows.append(window_ref[...].astype(F32))
    rows.append(jnp.zeros((out_ref.shape[2] - n_bands * (n_bands + 2) - 1, k_dev), F32))
    packed = jnp.concatenate(rows, axis=0)
    packed = jnp.concatenate([packed, jnp.zeros((packed.shape[0], 128 - k_dev), F32)], axis=1)
    packed = packed.T[:k_dev].astype(BF16)
    for d in range(out_ref.shape[0]):
        out_ref[d] = packed


def pack(eigvec, energies, window, copies):
    k_dev, n_bands, _ = eigvec.shape
    wide = -(-(n_bands * (n_bands + 2) + 1) // 128) * 128
    args = (eigvec.transpose(1, 2, 0), energies.T, window.reshape(1, k_dev))
    return pl.pallas_call(
        pack_kernel,
        grid=(1,),
        in_specs=[pl.BlockSpec(x.shape, lambda g, n=x.ndim: (0,) * n) for x in args],
        out_specs=pl.BlockSpec(memory_space=pltpu.VMEM),
        out_shape=pltpu.VMEM((copies, k_dev, wide), BF16),
        compiler_params=VMEM,
        name="pack_points",
    )(*[pltpu.with_memory_space_constraint(x, pltpu.HBM) for x in args])


def finish_kernel(n_bands, n_v, k_parts, place_ref, got_ref, el_out, ph_out, scr):
    n_ka, n_pb, n_row, rows, _ = got_ref.shape
    lane = iota((1, 128), 1)
    total = None
    for ka in range(n_ka):
        for pb in range(n_pb):
            for row in range(n_row):
                part = got_ref[ka, pb, row]
                total = part if total is None else total + part
    for x in range(K_PER):
        scr[pl.ds(x, rows, stride=K_PER), :] = pltpu.roll(total, 128 - n_bands * x, 1) if x else total
    k_dev = el_out.shape[1]
    mine = jnp.concatenate([scr[...], jnp.zeros((128 - k_dev, 128), F32)], axis=0)
    el_out[...] = mine.T[:n_bands, :k_dev]
    for row in range(n_row):
        line = jnp.zeros((1, 128), F32)
        for ka in range(n_ka):
            part = got_ref[ka, pl.ds(place_ref[0], 1), row][0]
            to = ka // k_parts * n_v
            moved = pltpu.roll(part[0:1], (to - K_PER * n_bands) % 128, 1)
            line = line + jnp.where((lane >= to) & (lane < to + n_v), moved, 0.0)
        ph_out[row : row + 1, :] = line[:, : ph_out.shape[1]]


def finish(got, place, n_bands, n_v, k_parts, k_dev, n_modes):
    n_row, rows = got.shape[2:4]
    el, ph = pl.pallas_call(
        functools.partial(finish_kernel, n_bands, n_v, k_parts),
        in_specs=[pl.BlockSpec(memory_space=pltpu.SMEM), pl.BlockSpec(memory_space=pltpu.VMEM)],
        out_shape=[
            jax.ShapeDtypeStruct((n_bands, k_dev), F32),
            jax.ShapeDtypeStruct((n_row, n_modes), F32),
        ],
        scratch_shapes=[pltpu.VMEM((rows * K_PER, 128), F32)],
        compiler_params=VMEM,
        name="finish",
    )(place, pltpu.with_memory_space_constraint(got, pltpu.VMEM))
    return el.T, ph


def rotate_kernel(n_modes, n_bands, v_parts, coup_ref, rot_ref, out_ref):
    r = coup_ref.shape[1]
    pair = n_bands * n_bands
    rows = n_modes * r
    x = coup_ref[0].astype(F32)
    x = jnp.concatenate([x[:, c * pair : (c + 1) * pair] for c in range(n_modes)], axis=0).astype(BF16)
    rot = rot_ref[...].astype(F32)
    rot = jnp.sum(jnp.where(iota(rot.shape, 1) == pl.program_id(0), rot, 0.0), axis=1).astype(BF16)
    spread_v = (iota((rows, n_modes), 0) // r == iota((rows, n_modes), 1)).astype(BF16)
    spread_c = (iota((n_modes, rows), 1) // r == iota((n_modes, rows), 0)).astype(BF16)
    half = lax.dot_general(spread_v, rot, (((1,), (1,)), ((), ())), preferred_element_type=F32)
    full = jnp.dot(half.astype(BF16), spread_c, preferred_element_type=F32)
    same = iota((rows, rows), 0) % r == iota((rows, rows), 1) % r
    big = jnp.where(same, full, 0.0).astype(BF16)
    y = jnp.dot(big, x, preferred_element_type=F32)
    n_v = n_modes // v_parts
    half_i = n_bands // 2
    wide = out_ref.shape[3]
    for part in range(v_parts):
        pieces = []
        for i in range(half_i):
            block = [
                y[v * r : (v + 1) * r, x * n_bands : (x + 1) * n_bands]
                for x in (i, i + half_i)
                for v in range(part * n_v, (part + 1) * n_v)
            ]
            if wide > 2 * n_v * n_bands:
                block.append(jnp.zeros((r, wide - 2 * n_v * n_bands), F32))
            pieces.append(jnp.concatenate(block, axis=1))
        out_ref[part, 0] = jnp.concatenate(pieces, axis=0).astype(BF16)


def rotate(coupling, rotation, n_bands, v_parts):
    q, r, width = coupling.shape
    n_modes = rotation.shape[1]
    rows = n_bands // 2 * r
    cols = -(-(2 * n_modes // v_parts * n_bands) // 128) * 128
    return pl.pallas_call(
        functools.partial(rotate_kernel, n_modes, n_bands, v_parts),
        grid=(q,),
        in_specs=[
            pl.BlockSpec((1, r, width), lambda a: (a, 0, 0)),
            pl.BlockSpec((n_modes, q, n_modes), lambda a: (0, 0, 0)),
        ],
        out_specs=pl.BlockSpec((v_parts, 1, rows, cols), lambda a: (0, a, 0, 0)),
        out_shape=jax.ShapeDtypeStruct((v_parts, q, rows, cols), BF16),
        compiler_params=VMEM,
        name="rotate_modes",
    )(
        pltpu.with_memory_space_constraint(coupling, pltpu.HBM),
        pltpu.with_memory_space_constraint(rotation.transpose(1, 0, 2), pltpu.HBM),
    )


def steps_of(k_loc):
    tiles = k_loc // (2 * K_PER)
    return tiles, -(-(tiles + 1) // UNROLL)


def prepare_kernel(
    n_bands, n_v, k_loc,
    freq_ref, start_ref, kq_ref, points_ref,
    wt_out, bd_out, gauss_out, occ_out,
    eig_scr, en_scr, keep_scr,
):
    g = pl.program_id(0)
    used = K_PER * n_bands
    k_all = points_ref.shape[0]
    at_en = points_ref.shape[1] - 128
    slots = 2 * K_PER
    scale = 1.0 / (SIGMA * math.sqrt(2.0))
    lane = iota((1, 128), 1)
    roll = lambda x, shift: pltpu.roll(x, shift % 128, 1) if shift % 128 else x

    @pl.when(g == 0)
    def _():
        en = roll(points_ref[:, at_en:].astype(F32), -(n_bands * n_bands % 128))
        lim = en[:, 2 * n_bands : 2 * n_bands + 1]
        en_scr[...] = jnp.where(lane < n_bands, en + roll(en, -n_bands), 0.0)
        keep = lane.astype(F32) < jnp.minimum(lim, float(n_bands))
        for i in range(n_bands):
            lo = i * n_bands
            tile = lo // 128 * 128
            block = roll(points_ref[:, tile : tile + 128].astype(F32), tile - lo)
            if lo + n_bands > tile + 128:
                more = roll(points_ref[:, tile + 128 : tile + 256].astype(F32), tile - lo)
                block = jnp.where(lane < tile + 128 - lo, block, more)
            eig_scr[pl.ds(i, k_all, stride=n_bands), :] = jnp.where(keep, block, 0.0)
        shape = (slots * n_bands, slots * n_bands)
        keep_scr[...] = (iota(shape, 0) // n_bands == iota(shape, 1) % slots).astype(BF16)

    by_band = (iota((n_bands, slots * n_bands), 0) == iota((n_bands, slots * n_bands), 1) // slots).astype(BF16)
    for step in range(PREPARED):
        t = g * PREPARED + step
        first = jnp.minimum(t * slots, k_loc - slots)
        v_tiles = []
        blocks = []
        for kg in range(2):
            vl = None
            level = None
            diagonal = []
            far_rows = []
            for x in range(K_PER):
                k = first + kg * K_PER + x
                near = k + start_ref[0]
                far = kq_ref[0, k]
                v = roll(eig_scr[pl.ds(pl.multiple_of(far * n_bands, 8), n_bands), :], n_bands * x)
                u = roll(eig_scr[pl.ds(pl.multiple_of(near * n_bands, 8), n_bands), :], n_bands * x)
                e = roll(en_scr[pl.ds(near, 1), :], n_bands * x)
                vl = v if vl is None else vl + v
                level = e if level is None else level + e
                diagonal.append(u)
                far_rows.append(jnp.broadcast_to(en_scr[pl.ds(far, 1), :], (n_bands, 128)))
            v_tiles.append(vl)
            blocks.append(jnp.concatenate(diagonal + [jnp.zeros((128 - used, 128), F32)], axis=0))
            cols = slice(kg * 128, (kg + 1) * 128)
            far_e = jnp.concatenate(far_rows + [jnp.zeros((128 - used, 128), F32)], axis=0).T[:n_bands]
            occ_out[step, :, cols] = jax.nn.sigmoid(-level / THERMAL_ENERGY_KT) - jax.nn.sigmoid(
                -far_e / THERMAL_ENERGY_KT
            )
            base = (far_e - level) * scale
            for v in range(0, n_v, 2):
                both = []
                for x in range(v, min(v + 2, n_v)):
                    d = base - freq_ref[0, x] * scale
                    both.append(jnp.exp(-(d * d)))
                rows = slice(v * n_bands, (v + len(both)) * n_bands)
                gauss_out[step, rows, cols] = jnp.concatenate(both, axis=0).astype(BF16)
        for kg in range(2):
            bd_out[step, kg] = blocks[kg].astype(BF16)
            turned = jnp.concatenate([blocks[kg][120:], blocks[kg][:120]], axis=0)
            bd_out[step, 2 + kg] = turned.astype(BF16)
        vl = jnp.concatenate(v_tiles, axis=1).astype(BF16)
        wt = lax.dot_general(vl, by_band, (((0,), (0,)), ((), ())), preferred_element_type=F32)
        wt = jnp.concatenate([wt[:used], wt[128 : 128 + used]], axis=0)
        wt_out[step] = wt.astype(BF16) * keep_scr[...]


def prepare(freq, start, kq, points, n_bands, n_v):
    k_loc = kq.shape[1]
    tiles, steps = steps_of(k_loc)
    tiles = max(tiles, steps * UNROLL)
    steps = -(-tiles // PREPARED)
    tiles = steps * PREPARED
    k_all = points.shape[0]
    wide = 2 * K_PER * n_bands
    smem = pl.BlockSpec(memory_space=pltpu.SMEM)
    shapes = ((wide, wide), (4, 128, 128), (n_v * n_bands, 256), (n_bands, 256))
    types = (BF16, BF16, BF16, F32)
    return pl.pallas_call(
        functools.partial(prepare_kernel, n_bands, n_v, k_loc),
        grid=(steps,),
        in_specs=[smem, smem, smem, pl.BlockSpec(memory_space=pltpu.VMEM)],
        out_specs=[
            pl.BlockSpec((PREPARED,) + x, lambda g, n=len(x): (g,) + (0,) * n) for x in shapes
        ],
        out_shape=[pltpu.HBM((tiles,) + x, t) for x, t in zip(shapes, types)],
        scratch_shapes=[
            pltpu.VMEM((k_all * n_bands, 128), F32),
            pltpu.VMEM((k_all, 128), F32),
            pltpu.VMEM((wide, wide), BF16),
        ],
        compiler_params=VMEM,
        name="prepare",
    )(freq, start, kq, points)


def swap_blocks(t_ref, n_bands, n_v):
    v_per = 128 // n_bands
    lane = iota((8, 128), 1)
    low = [n_bands * d % 128 for d in range(v_per + K_PER - 1)]
    from_low = [lane >= x for x in low]
    halves = [[[] for _ in range(v_per)] for _ in range(2)]
    for kg in range(2):
        for first in range(0, n_v, v_per):
            vg = first // v_per
            rolled = []
            for k in range(K_PER):
                row = (kg * K_PER + k) * n_bands
                block = t_ref[row : row + n_bands, vg * 128 : (vg + 1) * 128]
                rolled.append(pltpu.roll(block, n_bands * k, 1) if k else block)
            for x in range(min(v_per, n_v - first)):
                order = sorted(range(K_PER), key=lambda k: low[x + k])
                if low[x + order[-1]] + n_bands > 128:
                    order.insert(0, order[-1])
                for z in range(0, n_bands, 8):
                    mix = rolled[order[0]][z : z + 8]
                    for k in order[1:]:
                        mix = jnp.where(from_low[x + k], rolled[k][z : z + 8], mix)
                    halves[kg][x].append(mix)
    return [
        jnp.concatenate([jnp.concatenate(h[x], axis=0).astype(BF16) for h in halves], axis=1)
        for x in range(min(v_per, n_v))
    ]


def turned_blocks(bd_ref, x, n_bands):
    shift = n_bands * x % 128
    which = shift % 16 // 8
    shift -= 8 * which
    halves = []
    for kg in range(2):
        if shift:
            halves.append(
                jnp.concatenate(
                    [bd_ref[0, 2 * which + kg, 128 - shift :, :], bd_ref[0, 2 * which + kg, : 128 - shift, :]],
                    axis=0,
                )
            )
        else:
            halves.append(bd_ref[0, 2 * which + kg])
    zero = jnp.zeros((128, 128), BF16)
    return jnp.concatenate(
        [jnp.concatenate([halves[0], zero], axis=1), jnp.concatenate([zero, halves[1]], axis=1)], axis=0
    )


def tile_step(wt_ref, b_ref, t_new, t_old, bd_ref, gauss_ref, occ_ref, ph_scr, scale, n_bands, n_v):
    t_new[...] = jnp.dot(wt_ref[0], b_ref[0], preferred_element_type=F32)
    v_per = 128 // n_bands
    coupled = [
        jnp.dot(left, turned_blocks(bd_ref, x, n_bands), preferred_element_type=F32)
        for x, left in enumerate(swap_blocks(t_old, n_bands, n_v))
    ]
    occ = occ_ref[0]
    el = None
    for v in range(0, n_v, 2):
        count = min(2, n_v - v)
        gauss = gauss_ref[0, v * n_bands : (v + count) * n_bands, :].astype(F32)
        for x in range(count):
            at = (v + x) // v_per * n_bands
            c = coupled[(v + x) % v_per][at : at + n_bands]
            strength = c * c * gauss[x * n_bands : (x + 1) * n_bands]
            el = strength if el is None else el + strength
            weighed = strength * occ
            weighed = sum(weighed[z : z + 8] for z in range(0, n_bands, 8))
            weighed = weighed[:, :128] + weighed[:, 128:]
            ph_scr[v + x] += weighed if scale is None else weighed * scale
    el = jnp.sum(el, axis=0, keepdims=True)
    return [el[:, :128], el[:, 128:]]


def linewidth_kernel(n_bands, n_v, r, tiles, k_dev, el_scale, ph_scale, a_ref, phase_ref, *refs):
    refs = list(refs)
    take = lambda n: [refs.pop(0) for _ in range(n)]
    unroll = UNROLL
    sources = take(4)
    (send_out,) = take(1)
    held, (sems,) = take(4), take(1)
    wt_ref, bd_ref, gauss_ref, occ_ref = held
    (a_scr, b_scr, ph_scr, el_scr), t_scr = take(4), take(unroll)
    g = pl.program_id(0)
    last = pl.num_programs(0) - 1
    steps = -(-(tiles + 1) // unroll)
    n_src = a_ref.shape[0]
    half_i = n_bands // 2
    v_per = 128 // n_bands
    cols = n_v * n_bands
    slots = 2 * K_PER

    def copy(which, step):
        part = pl.ds(step * unroll, unroll)
        return pltpu.make_async_copy(sources[which].at[part], held[which].at[part], sems.at[which, step])

    @pl.when(g == 0)
    def _():
        for step in range(steps):
            for which in range(4):
                copy(which, step).start()
        lane = iota((1, 128), 1)
        for s in range(0, n_src, 2):
            for h in range(2):
                for vg in range(-(-n_v // v_per)):
                    lo = h * cols + vg * v_per * n_bands
                    tile, off = lo // 128 * 128, lo % 128
                    both = []
                    for x in (s, s + 1):
                        block = a_ref[x, :, tile : tile + 128].astype(F32)
                        if off:
                            block = pltpu.roll(block, 128 - off, 1)
                            if tile + 128 < a_ref.shape[2]:
                                more = a_ref[x, :, tile + 128 : tile + 256].astype(F32)
                                block = jnp.where(lane < 128 - off, block, pltpu.roll(more, 128 - off, 1))
                        both.append(block)
                    for i in range(half_i):
                        here = slice(i * r, (i + 1) * r)
                        a_scr[h * half_i + i, s * r : (s + 2) * r, vg * 128 : (vg + 1) * 128] = (
                            jnp.concatenate([both[0][here], both[1][here]], axis=0).astype(BF16)
                        )
        for i in range(0, n_bands, 2):
            b0 = jnp.dot(phase_ref[...], a_scr[i], preferred_element_type=F32)
            b1 = jnp.dot(phase_ref[...], a_scr[i + 1], preferred_element_type=F32)
            for t in range(tiles):
                here = slice(t * slots, (t + 1) * slots)
                b_scr[t, i * slots : (i + 2) * slots, :] = jnp.concatenate(
                    [b0[here], b1[here]], axis=0
                ).astype(BF16)
        t_scr[-1][...] = jnp.zeros_like(t_scr[-1])
        ph_scr[...] = jnp.zeros_like(ph_scr)

    for which in range(4):
        copy(which, g).wait()

    def tile_of(ref, n):
        return ref.at[pl.ds(jnp.clip(unroll * g + n, 0, tiles - 1), 1)]

    el = []
    for x in range(unroll):
        beyond = (steps - 1) * unroll + x - 1 >= tiles
        scale = jnp.where(g < last, 1.0, 0.0) if beyond else None
        el += tile_step(
            tile_of(wt_ref, x), tile_of(b_scr, x), t_scr[x], t_scr[x - 1], tile_of(bd_ref, x - 1),
            tile_of(gauss_ref, x - 1), tile_of(occ_ref, x - 1), ph_scr, scale, n_bands, n_v,
        )
    stride = el_scr.shape[0] // steps
    el_scr[pl.ds(g * stride, 2 * unroll), :] = jnp.concatenate(el, axis=0)

    @pl.when(g == last)
    def _():
        used = K_PER * n_bands
        n_ka, n_pb, n_row, n_rows, _ = send_out.shape
        sums = jnp.sum(ph_scr[...], axis=1)
        sums = jnp.concatenate([sums, jnp.zeros((128 - n_v, 128), F32)], axis=0).T
        sums = pltpu.roll(jnp.sum(sums, axis=0, keepdims=True) * ph_scale, used, 1)
        groups = [el_scr[x * stride : x * stride + 2 * unroll, :] for x in range(steps)]
        groups = jnp.concatenate(groups, axis=0) * el_scale
        lane = iota((n_rows, 128), 1)
        for d in range(n_ka * n_row):
            lo = 2 + d * n_rows
            part = jnp.where(lane < used, groups[lo : lo + n_rows], sums)
            for pb in range(n_pb):
                send_out[d // n_row, pb, d % n_row] = part


def linewidths(a, phase, prepared, k_loc, k_dev, n_row, n_pb, n_bands, n_v, r, el_scale, ph_scale):
    wt, bd, gauss, occ = prepared
    tiles, steps = steps_of(k_loc)
    lanes = -(-n_v // (128 // n_bands)) * 128
    wide = 2 * K_PER * n_bands
    depth = a.shape[0] * r
    a = pltpu.with_memory_space_constraint(a, pltpu.VMEM)
    tables = [pltpu.with_memory_space_constraint(x, pltpu.HBM) for x in (wt, bd, gauss, occ)]
    n_rows = k_dev // K_PER
    n_ka = k_loc // k_dev // n_row
    return pl.pallas_call(
        functools.partial(linewidth_kernel, n_bands, n_v, r, tiles, k_dev, el_scale, ph_scale),
        grid=(steps,),
        in_specs=[pl.BlockSpec(memory_space=pltpu.VMEM)] * 2
        + [pl.BlockSpec(memory_space=pltpu.HBM)] * len(tables),
        out_specs=pl.BlockSpec((n_ka, n_pb, n_row, n_rows, 128), lambda g: (0,) * 5),
        out_shape=jax.ShapeDtypeStruct((n_ka, n_pb, n_row, n_rows, 128), F32),
        scratch_shapes=[pltpu.VMEM(x.shape, x.dtype) for x in tables]
        + [pltpu.SemaphoreType.DMA((len(tables), steps))]
        + [
            pltpu.VMEM((n_bands, depth, lanes), BF16),
            pltpu.VMEM((tiles, wide, lanes), BF16),
            pltpu.VMEM((n_v, 8, 128), F32),
            pltpu.VMEM((steps * -(-2 * UNROLL // 8) * 8, 128), F32),
        ]
        + [pltpu.VMEM((wide, lanes), F32)] * UNROLL,
        compiler_params=VMEM,
        name="linewidths",
    )(a, phase, *tables)


def on_device(coupling, rotation, freq, eigvec, energies, window, kq_index, kpoints, lattice):
    plane = ("ka", "row")
    everywhere = ("ka", "pb", "row")
    n_ka = lax.axis_size("ka")
    n_row = lax.axis_size("row")
    n_pb = lax.axis_size("pb")
    n_group = n_ka * n_row
    k_dev, n_bands = eigvec.shape[:2]
    q_dev, n_modes = rotation.shape[:2]
    assert q_dev == n_row
    pair = n_bands * n_bands
    total_k = k_dev * n_group
    total_q = q_dev * n_pb
    v_parts = math.gcd(n_modes, n_ka)
    k_parts = n_ka // v_parts
    n_v = n_modes // v_parts
    k_loc = total_k // k_parts
    ka_pos = lax.axis_index("ka")
    row_pos = lax.axis_index("row")
    pb_pos = lax.axis_index("pb")

    points = pack(eigvec, energies, window, n_group)
    points = lax.all_to_all(points, plane, 0, 0, tiled=True).reshape(total_k, -1)

    pad = -coupling.shape[1] % 8
    if pad:
        coupling = jnp.pad(coupling, ((0, 0), (0, pad), (0, 0)))
    r = coupling.shape[1]
    rotated = rotate(coupling, rotation, n_bands, v_parts)
    if k_parts > 1:
        rotated = jnp.repeat(rotated, k_parts, axis=0)
    rotated = rotated.reshape((n_group,) + rotated.shape[2:])
    a = lax.all_to_all(rotated, plane, 0, 0, tiled=True)
    k_start = (ka_pos % k_parts) * k_loc
    kp = lax.dynamic_slice_in_dim(kpoints, k_start, k_loc, 0)
    phase = phase_rows(lattice, kp)
    if pad:
        phase = jnp.pad(phase.reshape(k_loc, n_group, r - pad), ((0, 0), (0, 0), (0, pad)))
        phase = phase.reshape(k_loc, n_group * r)
    kq = lax.dynamic_slice(kq_index, (row_pos, k_start), (1, k_loc))
    v_start = (ka_pos // k_parts) * n_v
    freq_mine = lax.dynamic_slice(freq, (row_pos, v_start), (1, n_v))
    points = pltpu.with_memory_space_constraint(points, pltpu.VMEM)
    prepared = prepare(freq_mine, k_start[None], kq, points, n_bands, n_v)
    norm = 1.0 / (math.sqrt(2.0 * math.pi) * SIGMA)
    send = linewidths(
        a, phase, prepared, k_loc, k_dev, n_row, n_pb, n_bands, n_v, r,
        norm / (total_q * n_modes * n_bands), norm / (total_k * n_bands),
    )
    if k_parts > 1:
        used = K_PER * n_bands
        rest = jnp.where(jnp.arange(128) < used, 0.0, send[:1])
        rest = jnp.broadcast_to(rest, (n_ka,) + send.shape[1:])
        send = lax.dynamic_update_slice_in_dim(rest, send, k_start // (k_dev * n_row), 0)
    got = lax.all_to_all(
        send.reshape((n_group * n_pb,) + send.shape[3:]), everywhere, 0, 0, tiled=True
    ).reshape(send.shape)
    place = pb_pos[None].astype(jnp.int32)
    electron, phonon = finish(got, place, n_bands, n_v, k_parts, k_dev, n_modes)
    return (electron, phonon)


def solution(mesh):
    return jax.shard_map(
        on_device,
        mesh=mesh,
        in_specs=(
            P("pb", ("ka", "row"), None),
            P("pb", None, None),
            P("pb", None),
            P(("ka", "row"), None, None),
            P(("ka", "row"), None),
            P(("ka", "row")),
            P("pb", None),
            P(),
            P(),
        ),
        out_specs=(P(("ka", "row"), None), P("pb", None)),
        check_vma=False,
    )
```

```python
import functools
import math

import jax
import jax.numpy as jnp
import numpy as np
from jax import lax
from jax.experimental import pallas as pl
from jax.experimental.pallas import tpu as pltpu
from jax.sharding import PartitionSpec as P

SIGMA = 0.1
THERMAL_ENERGY_KT = 0.2
VMEM = pltpu.CompilerParams(vmem_limit_bytes=40 * 1024 * 1024)
F32 = jnp.float32
BF16 = jnp.bfloat16
UNROLL = 11
PREPARED = 3
K_PER = 4


def phase_rows(lattice, kpoint_rows):
    rvec = lattice.astype(jnp.float32)
    argument = (
        rvec[:, 0][None, :] * kpoint_rows[:, 0:1]
        + rvec[:, 1][None, :] * kpoint_rows[:, 1:2]
        + rvec[:, 2][None, :] * kpoint_rows[:, 2:3]
    )
    return jnp.cos(2.0 * math.pi * argument).astype(jnp.bfloat16)


def iota(shape, dim):
    return lax.broadcasted_iota(jnp.int32, shape, dim)


def pack_kernel(eig_ref, en_ref, window_ref, out_ref):
    n_bands, _, k_dev = eig_ref.shape
    rest = en_ref[...]
    high = rest.astype(BF16).astype(F32)
    rows = [eig_ref[...].astype(F32).reshape(n_bands * n_bands, k_dev), high, rest - high]
    rows.append(window_ref[...].astype(F32))
    rows.append(jnp.zeros((out_ref.shape[2] - n_bands * (n_bands + 2) - 1, k_dev), F32))
    packed = jnp.concatenate(rows, axis=0)
    packed = jnp.concatenate([packed, jnp.zeros((packed.shape[0], 128 - k_dev), F32)], axis=1)
    packed = packed.T[:k_dev].astype(BF16)
    half = k_dev // 2
    for d in range(out_ref.shape[0]):
        out_ref[d] = packed[d % 2 * half : (d % 2 + 1) * half]


def pack(eigvec, energies, window, copies):
    k_dev, n_bands, _ = eigvec.shape
    wide = -(-(n_bands * (n_bands + 2) + 1) // 128) * 128
    args = (eigvec.transpose(1, 2, 0), energies.T, window.reshape(1, k_dev))
    return pl.pallas_call(
        pack_kernel,
        grid=(1,),
        in_specs=[pl.BlockSpec(x.shape, lambda g, n=x.ndim: (0,) * n) for x in args],
        out_specs=pl.BlockSpec(memory_space=pltpu.VMEM),
        out_shape=pltpu.VMEM((copies, k_dev // 2, wide), BF16),
        compiler_params=VMEM,
        name="pack_points",
    )(*[pltpu.with_memory_space_constraint(x, pltpu.HBM) for x in args])


def finish_kernel(n_bands, n_v, k_parts, place_ref, got_ref, el_out, ph_out, scr):
    n_ka, n_pb, n_row, rows, _ = got_ref.shape
    lane = iota((1, 128), 1)
    total = None
    for ka in range(n_ka):
        for pb in range(n_pb):
            for row in range(n_row):
                part = got_ref[ka, pb, row]
                total = part if total is None else total + part
    for x in range(K_PER):
        scr[pl.ds(x, rows, stride=K_PER), :] = pltpu.roll(total, 128 - n_bands * x, 1) if x else total
    k_dev = el_out.shape[1]
    mine = jnp.concatenate([scr[...], jnp.zeros((128 - k_dev, 128), F32)], axis=0)
    el_out[...] = mine.T[:n_bands, :k_dev]
    for row in range(n_row):
        line = jnp.zeros((1, 128), F32)
        for ka in range(n_ka):
            part = got_ref[ka, pl.ds(place_ref[0], 1), row][0]
            to = ka // k_parts * n_v
            moved = pltpu.roll(part[0:1], (to - K_PER * n_bands) % 128, 1)
            line = line + jnp.where((lane >= to) & (lane < to + n_v), moved, 0.0)
        ph_out[row : row + 1, :] = line[:, : ph_out.shape[1]]


def finish(got, place, n_bands, n_v, k_parts, k_dev, n_modes):
    n_row, rows = got.shape[2:4]
    el, ph = pl.pallas_call(
        functools.partial(finish_kernel, n_bands, n_v, k_parts),
        in_specs=[pl.BlockSpec(memory_space=pltpu.SMEM), pl.BlockSpec(memory_space=pltpu.VMEM)],
        out_shape=[
            jax.ShapeDtypeStruct((n_bands, k_dev), F32),
            jax.ShapeDtypeStruct((n_row, n_modes), F32),
        ],
        scratch_shapes=[pltpu.VMEM((rows * K_PER, 128), F32)],
        compiler_params=VMEM,
        name="finish",
    )(place, pltpu.with_memory_space_constraint(got, pltpu.VMEM))
    return el.T, ph


def rotate_kernel(n_modes, n_bands, v_parts, coup_ref, rot_ref, out_ref):
    r = coup_ref.shape[1]
    pair = n_bands * n_bands
    rows = n_modes * r
    x = coup_ref[0].astype(F32)
    x = jnp.concatenate([x[:, c * pair : (c + 1) * pair] for c in range(n_modes)], axis=0).astype(BF16)
    rot = rot_ref[...].astype(F32)
    rot = jnp.sum(jnp.where(iota(rot.shape, 1) == pl.program_id(0), rot, 0.0), axis=1).astype(BF16)
    spread_v = (iota((rows, n_modes), 0) // r == iota((rows, n_modes), 1)).astype(BF16)
    spread_c = (iota((n_modes, rows), 1) // r == iota((n_modes, rows), 0)).astype(BF16)
    half = lax.dot_general(spread_v, rot, (((1,), (1,)), ((), ())), preferred_element_type=F32)
    full = jnp.dot(half.astype(BF16), spread_c, preferred_element_type=F32)
    same = iota((rows, rows), 0) % r == iota((rows, rows), 1) % r
    big = jnp.where(same, full, 0.0).astype(BF16)
    y = jnp.dot(big, x, preferred_element_type=F32)
    n_v = n_modes // v_parts
    half_i = n_bands // 2
    wide = out_ref.shape[3]
    for part in range(v_parts):
        pieces = []
        for i in range(half_i):
            block = [
                y[v * r : (v + 1) * r, x * n_bands : (x + 1) * n_bands]
                for x in (i, i + half_i)
                for v in range(part * n_v, (part + 1) * n_v)
            ]
            if wide > 2 * n_v * n_bands:
                block.append(jnp.zeros((r, wide - 2 * n_v * n_bands), F32))
            pieces.append(jnp.concatenate(block, axis=1))
        out_ref[part, 0] = jnp.concatenate(pieces, axis=0).astype(BF16)


def rotate(coupling, rotation, n_bands, v_parts):
    q, r, width = coupling.shape
    n_modes = rotation.shape[1]
    rows = n_bands // 2 * r
    cols = -(-(2 * n_modes // v_parts * n_bands) // 128) * 128
    return pl.pallas_call(
        functools.partial(rotate_kernel, n_modes, n_bands, v_parts),
        grid=(q,),
        in_specs=[
            pl.BlockSpec((1, r, width), lambda a: (a, 0, 0)),
            pl.BlockSpec((n_modes, q, n_modes), lambda a: (0, 0, 0)),
        ],
        out_specs=pl.BlockSpec((v_parts, 1, rows, cols), lambda a: (0, a, 0, 0)),
        out_shape=jax.ShapeDtypeStruct((v_parts, q, rows, cols), BF16),
        compiler_params=VMEM,
        name="rotate_modes",
    )(
        pltpu.with_memory_space_constraint(coupling, pltpu.HBM),
        pltpu.with_memory_space_constraint(rotation.transpose(1, 0, 2), pltpu.HBM),
    )


def steps_of(k_loc):
    tiles = k_loc // (2 * K_PER)
    return tiles, -(-(tiles + 1) // UNROLL)


def prepare_kernel(
    n_bands, n_v, k_loc,
    freq_ref, start_ref, kq_ref, points_ref,
    wt_out, bd_out, gauss_out, occ_out,
    eig_scr, en_scr, keep_scr,
):
    g = pl.program_id(0)
    used = K_PER * n_bands
    k_all = points_ref.shape[0]
    at_en = points_ref.shape[1] - 128
    slots = 2 * K_PER
    scale = 1.0 / (SIGMA * math.sqrt(2.0))
    lane = iota((1, 128), 1)
    roll = lambda x, shift: pltpu.roll(x, shift % 128, 1) if shift % 128 else x

    @pl.when(g == 0)
    def _():
        en = roll(points_ref[:, at_en:].astype(F32), -(n_bands * n_bands % 128))
        lim = en[:, 2 * n_bands : 2 * n_bands + 1]
        en_scr[...] = jnp.where(lane < n_bands, en + roll(en, -n_bands), 0.0)
        keep = lane.astype(F32) < jnp.minimum(lim, float(n_bands))
        for i in range(n_bands):
            lo = i * n_bands
            tile = lo // 128 * 128
            block = roll(points_ref[:, tile : tile + 128].astype(F32), tile - lo)
            if lo + n_bands > tile + 128:
                more = roll(points_ref[:, tile + 128 : tile + 256].astype(F32), tile - lo)
                block = jnp.where(lane < tile + 128 - lo, block, more)
            eig_scr[pl.ds(i, k_all, stride=n_bands), :] = jnp.where(keep, block, 0.0)
        shape = (slots * n_bands, slots * n_bands)
        keep_scr[...] = (iota(shape, 0) // n_bands == iota(shape, 1) % slots).astype(BF16)

    by_band = (iota((n_bands, slots * n_bands), 0) == iota((n_bands, slots * n_bands), 1) // slots).astype(BF16)
    for step in range(PREPARED):
        t = g * PREPARED + step
        first = jnp.minimum(t * slots, k_loc - slots)
        v_tiles = []
        blocks = []
        for kg in range(2):
            vl = None
            level = None
            diagonal = []
            far_rows = []
            for x in range(K_PER):
                k = first + kg * K_PER + x
                near = k + start_ref[0]
                far = kq_ref[0, k]
                v = roll(eig_scr[pl.ds(pl.multiple_of(far * n_bands, 8), n_bands), :], n_bands * x)
                u = roll(eig_scr[pl.ds(pl.multiple_of(near * n_bands, 8), n_bands), :], n_bands * x)
                e = roll(en_scr[pl.ds(near, 1), :], n_bands * x)
                vl = v if vl is None else vl + v
                level = e if level is None else level + e
                diagonal.append(u)
                far_rows.append(jnp.broadcast_to(en_scr[pl.ds(far, 1), :], (n_bands, 128)))
            v_tiles.append(vl)
            blocks.append(jnp.concatenate(diagonal + [jnp.zeros((128 - used, 128), F32)], axis=0))
            cols = slice(kg * 128, (kg + 1) * 128)
            far_e = jnp.concatenate(far_rows + [jnp.zeros((128 - used, 128), F32)], axis=0).T[:n_bands]
            occ_out[step, :, cols] = jax.nn.sigmoid(-level / THERMAL_ENERGY_KT) - jax.nn.sigmoid(
                -far_e / THERMAL_ENERGY_KT
            )
            base = (far_e - level) * scale
            for v in range(0, n_v, 2):
                both = []
                for x in range(v, min(v + 2, n_v)):
                    d = base - freq_ref[0, x] * scale
                    both.append(jnp.exp(-(d * d)))
                rows = slice(v * n_bands, (v + len(both)) * n_bands)
                gauss_out[step, rows, cols] = jnp.concatenate(both, axis=0).astype(BF16)
        for kg in range(2):
            bd_out[step, kg] = blocks[kg].astype(BF16)
            turned = jnp.concatenate([blocks[kg][120:], blocks[kg][:120]], axis=0)
            bd_out[step, 2 + kg] = turned.astype(BF16)
        vl = jnp.concatenate(v_tiles, axis=1).astype(BF16)
        wt = lax.dot_general(vl, by_band, (((0,), (0,)), ((), ())), preferred_element_type=F32)
        wt = jnp.concatenate([wt[:used], wt[128 : 128 + used]], axis=0)
        wt_out[step] = wt.astype(BF16) * keep_scr[...]


def prepare(freq, start, kq, points, n_bands, n_v):
    k_loc = kq.shape[1]
    tiles, steps = steps_of(k_loc)
    tiles = max(tiles, steps * UNROLL)
    steps = -(-tiles // PREPARED)
    tiles = steps * PREPARED
    k_all = points.shape[0]
    wide = 2 * K_PER * n_bands
    smem = pl.BlockSpec(memory_space=pltpu.SMEM)
    shapes = ((wide, wide), (4, 128, 128), (n_v * n_bands, 256), (n_bands, 256))
    types = (BF16, BF16, BF16, F32)
    return pl.pallas_call(
        functools.partial(prepare_kernel, n_bands, n_v, k_loc),
        grid=(steps,),
        in_specs=[smem, smem, smem, pl.BlockSpec(memory_space=pltpu.VMEM)],
        out_specs=[
            pl.BlockSpec((PREPARED,) + x, lambda g, n=len(x): (g,) + (0,) * n) for x in shapes
        ],
        out_shape=[pltpu.HBM((tiles,) + x, t) for x, t in zip(shapes, types)],
        scratch_shapes=[
            pltpu.VMEM((k_all * n_bands, 128), F32),
            pltpu.VMEM((k_all, 128), F32),
            pltpu.VMEM((wide, wide), BF16),
        ],
        compiler_params=VMEM,
        name="prepare",
    )(freq, start, kq, points)


def swap_blocks(t_ref, n_bands, n_v):
    v_per = 128 // n_bands
    lane = iota((8, 128), 1)
    low = [n_bands * d % 128 for d in range(v_per + K_PER - 1)]
    from_low = [lane >= x for x in low]
    halves = [[[] for _ in range(v_per)] for _ in range(2)]
    for kg in range(2):
        for first in range(0, n_v, v_per):
            vg = first // v_per
            rolled = []
            for k in range(K_PER):
                row = (kg * K_PER + k) * n_bands
                block = t_ref[row : row + n_bands, vg * 128 : (vg + 1) * 128]
                rolled.append(pltpu.roll(block, n_bands * k, 1) if k else block)
            for x in range(min(v_per, n_v - first)):
                order = sorted(range(K_PER), key=lambda k: low[x + k])
                if low[x + order[-1]] + n_bands > 128:
                    order.insert(0, order[-1])
                for z in range(0, n_bands, 8):
                    mix = rolled[order[0]][z : z + 8]
                    for k in order[1:]:
                        mix = jnp.where(from_low[x + k], rolled[k][z : z + 8], mix)
                    halves[kg][x].append(mix)
    return [
        jnp.concatenate([jnp.concatenate(h[x], axis=0).astype(BF16) for h in halves], axis=1)
        for x in range(min(v_per, n_v))
    ]


def turned_blocks(bd_ref, x, n_bands):
    shift = n_bands * x % 128
    which = shift % 16 // 8
    shift -= 8 * which
    halves = []
    for kg in range(2):
        if shift:
            halves.append(
                jnp.concatenate(
                    [bd_ref[0, 2 * which + kg, 128 - shift :, :], bd_ref[0, 2 * which + kg, : 128 - shift, :]],
                    axis=0,
                )
            )
        else:
            halves.append(bd_ref[0, 2 * which + kg])
    zero = jnp.zeros((128, 128), BF16)
    return jnp.concatenate(
        [jnp.concatenate([halves[0], zero], axis=1), jnp.concatenate([zero, halves[1]], axis=1)], axis=0
    )


def tile_step(wt_ref, b_ref, t_new, t_old, bd_ref, gauss_ref, occ_ref, ph_scr, scale, n_bands, n_v):
    t_new[...] = jnp.dot(wt_ref[0], b_ref[0], preferred_element_type=F32)
    v_per = 128 // n_bands
    coupled = [
        jnp.dot(left, turned_blocks(bd_ref, x, n_bands), preferred_element_type=F32)
        for x, left in enumerate(swap_blocks(t_old, n_bands, n_v))
    ]
    occ = occ_ref[0]
    el = None
    for v in range(0, n_v, 2):
        count = min(2, n_v - v)
        gauss = gauss_ref[0, v * n_bands : (v + count) * n_bands, :].astype(F32)
        for x in range(count):
            at = (v + x) // v_per * n_bands
            c = coupled[(v + x) % v_per][at : at + n_bands]
            strength = c * c * gauss[x * n_bands : (x + 1) * n_bands]
            el = strength if el is None else el + strength
            weighed = strength * occ
            weighed = sum(weighed[z : z + 8] for z in range(0, n_bands, 8))
            weighed = weighed[:, :128] + weighed[:, 128:]
            ph_scr[v + x] += weighed if scale is None else weighed * scale
    el = jnp.sum(el, axis=0, keepdims=True)
    return [el[:, :128], el[:, 128:]]


def linewidth_kernel(n_bands, n_v, r, tiles, k_dev, el_scale, ph_scale, a_ref, phase_ref, *refs):
    refs = list(refs)
    take = lambda n: [refs.pop(0) for _ in range(n)]
    unroll = UNROLL
    sources = take(4)
    (send_out,) = take(1)
    held, (sems,) = take(4), take(1)
    wt_ref, bd_ref, gauss_ref, occ_ref = held
    (a_scr, b_scr, ph_scr, el_scr), t_scr = take(4), take(unroll)
    g = pl.program_id(0)
    last = pl.num_programs(0) - 1
    steps = -(-(tiles + 1) // unroll)
    n_src = a_ref.shape[0]
    half_i = n_bands // 2
    v_per = 128 // n_bands
    cols = n_v * n_bands
    slots = 2 * K_PER

    def copy(which, step):
        part = pl.ds(step * unroll, unroll)
        return pltpu.make_async_copy(sources[which].at[part], held[which].at[part], sems.at[which, step])

    @pl.when(g == 0)
    def _():
        for step in range(steps):
            for which in range(4):
                copy(which, step).start()
        lane = iota((1, 128), 1)
        for s in range(0, n_src, 2):
            for h in range(2):
                for vg in range(-(-n_v // v_per)):
                    lo = h * cols + vg * v_per * n_bands
                    tile, off = lo // 128 * 128, lo % 128
                    both = []
                    for x in (s, s + 1):
                        block = a_ref[x, :, tile : tile + 128].astype(F32)
                        if off:
                            block = pltpu.roll(block, 128 - off, 1)
                            if tile + 128 < a_ref.shape[2]:
                                more = a_ref[x, :, tile + 128 : tile + 256].astype(F32)
                                block = jnp.where(lane < 128 - off, block, pltpu.roll(more, 128 - off, 1))
                        both.append(block)
                    for i in range(half_i):
                        here = slice(i * r, (i + 1) * r)
                        a_scr[h * half_i + i, s * r : (s + 2) * r, vg * 128 : (vg + 1) * 128] = (
                            jnp.concatenate([both[0][here], both[1][here]], axis=0).astype(BF16)
                        )
        for i in range(0, n_bands, 2):
            b0 = jnp.dot(phase_ref[...], a_scr[i], preferred_element_type=F32)
            b1 = jnp.dot(phase_ref[...], a_scr[i + 1], preferred_element_type=F32)
            for t in range(tiles):
                here = slice(t * slots, (t + 1) * slots)
                b_scr[t, i * slots : (i + 2) * slots, :] = jnp.concatenate(
                    [b0[here], b1[here]], axis=0
                ).astype(BF16)
        t_scr[-1][...] = jnp.zeros_like(t_scr[-1])
        ph_scr[...] = jnp.zeros_like(ph_scr)

    for which in range(4):
        copy(which, g).wait()

    def tile_of(ref, n):
        return ref.at[pl.ds(jnp.clip(unroll * g + n, 0, tiles - 1), 1)]

    el = []
    for x in range(unroll):
        beyond = (steps - 1) * unroll + x - 1 >= tiles
        scale = jnp.where(g < last, 1.0, 0.0) if beyond else None
        el += tile_step(
            tile_of(wt_ref, x), tile_of(b_scr, x), t_scr[x], t_scr[x - 1], tile_of(bd_ref, x - 1),
            tile_of(gauss_ref, x - 1), tile_of(occ_ref, x - 1), ph_scr, scale, n_bands, n_v,
        )
    stride = el_scr.shape[0] // steps
    el_scr[pl.ds(g * stride, 2 * unroll), :] = jnp.concatenate(el, axis=0)

    @pl.when(g == last)
    def _():
        used = K_PER * n_bands
        n_ka, n_pb, n_row, n_rows, _ = send_out.shape
        sums = jnp.sum(ph_scr[...], axis=1)
        sums = jnp.concatenate([sums, jnp.zeros((128 - n_v, 128), F32)], axis=0).T
        sums = pltpu.roll(jnp.sum(sums, axis=0, keepdims=True) * ph_scale, used, 1)
        groups = [el_scr[x * stride : x * stride + 2 * unroll, :] for x in range(steps)]
        groups = jnp.concatenate(groups, axis=0) * el_scale
        lane = iota((n_rows, 128), 1)
        for d in range(n_ka * n_row):
            lo = 2 + d * n_rows
            part = jnp.where(lane < used, groups[lo : lo + n_rows], sums)
            for pb in range(n_pb):
                send_out[d // n_row, pb, d % n_row] = part


def linewidths(a, phase, prepared, k_loc, k_dev, n_row, n_pb, n_bands, n_v, r, el_scale, ph_scale):
    wt, bd, gauss, occ = prepared
    tiles, steps = steps_of(k_loc)
    lanes = -(-n_v // (128 // n_bands)) * 128
    wide = 2 * K_PER * n_bands
    depth = a.shape[0] * r
    a = pltpu.with_memory_space_constraint(a, pltpu.VMEM)
    tables = [pltpu.with_memory_space_constraint(x, pltpu.HBM) for x in (wt, bd, gauss, occ)]
    n_rows = k_dev // K_PER
    n_ka = k_loc // k_dev // n_row
    return pl.pallas_call(
        functools.partial(linewidth_kernel, n_bands, n_v, r, tiles, k_dev, el_scale, ph_scale),
        grid=(steps,),
        in_specs=[pl.BlockSpec(memory_space=pltpu.VMEM)] * 2
        + [pl.BlockSpec(memory_space=pltpu.HBM)] * len(tables),
        out_specs=pl.BlockSpec((n_ka, n_pb, n_row, n_rows, 128), lambda g: (0,) * 5),
        out_shape=jax.ShapeDtypeStruct((n_ka, n_pb, n_row, n_rows, 128), F32),
        scratch_shapes=[pltpu.VMEM(x.shape, x.dtype) for x in tables]
        + [pltpu.SemaphoreType.DMA((len(tables), steps))]
        + [
            pltpu.VMEM((n_bands, depth, lanes), BF16),
            pltpu.VMEM((tiles, wide, lanes), BF16),
            pltpu.VMEM((n_v, 8, 128), F32),
            pltpu.VMEM((steps * -(-2 * UNROLL // 8) * 8, 128), F32),
        ]
        + [pltpu.VMEM((wide, lanes), F32)] * UNROLL,
        compiler_params=VMEM,
        name="linewidths",
    )(a, phase, *tables)


def on_device(coupling, rotation, freq, eigvec, energies, window, kq_index, kpoints, lattice):
    plane = ("ka", "row")
    everywhere = ("ka", "pb", "row")
    n_ka = lax.axis_size("ka")
    n_row = lax.axis_size("row")
    n_pb = lax.axis_size("pb")
    n_group = n_ka * n_row
    k_dev, n_bands = eigvec.shape[:2]
    q_dev, n_modes = rotation.shape[:2]
    assert q_dev == n_row
    pair = n_bands * n_bands
    total_k = k_dev * n_group
    total_q = q_dev * n_pb
    v_parts = math.gcd(n_modes, n_ka)
    k_parts = n_ka // v_parts
    n_v = n_modes // v_parts
    k_loc = total_k // k_parts
    ka_pos = lax.axis_index("ka")
    row_pos = lax.axis_index("row")
    pb_pos = lax.axis_index("pb")

    points = pack(eigvec, energies, window, n_group)
    mine = lax.all_to_all(points, plane, 0, 0, tiled=True)
    other = lax.ppermute(mine, "row", [(i, i ^ 1) for i in range(n_row)])
    odd = row_pos % 2 == 1
    points = jnp.concatenate([jnp.where(odd, other, mine), jnp.where(odd, mine, other)], axis=1)
    points = points.reshape(total_k, -1)

    pad = -coupling.shape[1] % 8
    if pad:
        coupling = jnp.pad(coupling, ((0, 0), (0, pad), (0, 0)))
    r = coupling.shape[1]
    rotated = rotate(coupling, rotation, n_bands, v_parts)
    if k_parts > 1:
        rotated = jnp.repeat(rotated, k_parts, axis=0)
    rotated = rotated.reshape((n_group,) + rotated.shape[2:])
    a = lax.all_to_all(rotated, plane, 0, 0, tiled=True)
    k_start = (ka_pos % k_parts) * k_loc
    kp = lax.dynamic_slice_in_dim(kpoints, k_start, k_loc, 0)
    phase = phase_rows(lattice, kp)
    if pad:
        phase = jnp.pad(phase.reshape(k_loc, n_group, r - pad), ((0, 0), (0, 0), (0, pad)))
        phase = phase.reshape(k_loc, n_group * r)
    kq = lax.dynamic_slice(kq_index, (row_pos, k_start), (1, k_loc))
    v_start = (ka_pos // k_parts) * n_v
    freq_mine = lax.dynamic_slice(freq, (row_pos, v_start), (1, n_v))
    points = pltpu.with_memory_space_constraint(points, pltpu.VMEM)
    prepared = prepare(freq_mine, k_start[None], kq, points, n_bands, n_v)
    norm = 1.0 / (math.sqrt(2.0 * math.pi) * SIGMA)
    send = linewidths(
        a, phase, prepared, k_loc, k_dev, n_row, n_pb, n_bands, n_v, r,
        norm / (total_q * n_modes * n_bands), norm / (total_k * n_bands),
    )
    if k_parts > 1:
        used = K_PER * n_bands
        rest = jnp.where(jnp.arange(128) < used, 0.0, send[:1])
        rest = jnp.broadcast_to(rest, (n_ka,) + send.shape[1:])
        send = lax.dynamic_update_slice_in_dim(rest, send, k_start // (k_dev * n_row), 0)
    got = lax.all_to_all(
        send.reshape((n_group * n_pb,) + send.shape[3:]), everywhere, 0, 0, tiled=True
    ).reshape(send.shape)
    place = pb_pos[None].astype(jnp.int32)
    electron, phonon = finish(got, place, n_bands, n_v, k_parts, k_dev, n_modes)
    return (electron, phonon)


def solution(mesh):
    return jax.shard_map(
        on_device,
        mesh=mesh,
        in_specs=(
            P("pb", ("ka", "row"), None),
            P("pb", None, None),
            P("pb", None),
            P(("ka", "row"), None, None),
            P(("ka", "row"), None),
            P(("ka", "row")),
            P("pb", None),
            P(),
            P(),
        ),
        out_specs=(P(("ka", "row"), None), P("pb", None)),
        check_vma=False,
    )
```

```python
import functools
import math

import jax
import jax.numpy as jnp
import numpy as np
from jax import lax
from jax.experimental import pallas as pl
from jax.experimental.pallas import tpu as pltpu
from jax.sharding import PartitionSpec as P

SIGMA = 0.1
THERMAL_ENERGY_KT = 0.2
VMEM = pltpu.CompilerParams(vmem_limit_bytes=40 * 1024 * 1024)
F32 = jnp.float32
BF16 = jnp.bfloat16
UNROLL = 11
PREPARED = 3
K_PER = 4
I_ROWS = 2


def phase_rows(lattice, kpoint_rows):
    rvec = lattice.astype(jnp.float32)
    argument = (
        rvec[:, 0][None, :] * kpoint_rows[:, 0:1]
        + rvec[:, 1][None, :] * kpoint_rows[:, 1:2]
        + rvec[:, 2][None, :] * kpoint_rows[:, 2:3]
    )
    return jnp.cos(2.0 * math.pi * argument).astype(jnp.bfloat16)


def iota(shape, dim):
    return lax.broadcasted_iota(jnp.int32, shape, dim)


def pack_kernel(eig_ref, en_ref, window_ref, out_ref):
    n_bands, _, k_dev = eig_ref.shape
    rest = en_ref[...]
    high = rest.astype(BF16).astype(F32)
    rows = [eig_ref[...].astype(F32).reshape(n_bands * n_bands, k_dev), high, rest - high]
    rows.append(window_ref[...].astype(F32))
    rows.append(jnp.zeros((out_ref.shape[2] - n_bands * (n_bands + 2) - 1, k_dev), F32))
    packed = jnp.concatenate(rows, axis=0)
    packed = jnp.concatenate([packed, jnp.zeros((packed.shape[0], 128 - k_dev), F32)], axis=1)
    packed = packed.T[:k_dev].astype(BF16)
    half = k_dev // 2
    for d in range(out_ref.shape[0]):
        out_ref[d] = packed[d % 2 * half : (d % 2 + 1) * half]


def pack(eigvec, energies, window, copies):
    k_dev, n_bands, _ = eigvec.shape
    wide = -(-(n_bands * (n_bands + 2) + 1) // 128) * 128
    args = (eigvec.transpose(1, 2, 0), energies.T, window.reshape(1, k_dev))
    return pl.pallas_call(
        pack_kernel,
        grid=(1,),
        in_specs=[pl.BlockSpec(x.shape, lambda g, n=x.ndim: (0,) * n) for x in args],
        out_specs=pl.BlockSpec(memory_space=pltpu.VMEM),
        out_shape=pltpu.VMEM((copies, k_dev // 2, wide), BF16),
        compiler_params=VMEM,
        name="pack_points",
    )(*[pltpu.with_memory_space_constraint(x, pltpu.HBM) for x in args])


def finish_kernel(n_bands, n_v, k_parts, place_ref, got_ref, el_out, ph_out, scr):
    n_ka, n_pb, n_row, rows, _ = got_ref.shape
    lane = iota((1, 128), 1)
    total = None
    for ka in range(n_ka):
        for pb in range(n_pb):
            for row in range(n_row):
                part = got_ref[ka, pb, row]
                total = part if total is None else total + part
    for x in range(K_PER):
        scr[pl.ds(x, rows, stride=K_PER), :] = pltpu.roll(total, 128 - n_bands * x, 1) if x else total
    k_dev = el_out.shape[1]
    mine = jnp.concatenate([scr[...], jnp.zeros((128 - k_dev, 128), F32)], axis=0)
    el_out[...] = mine.T[:n_bands, :k_dev]
    for row in range(n_row):
        line = jnp.zeros((1, 128), F32)
        for ka in range(n_ka):
            part = got_ref[ka, pl.ds(place_ref[0], 1), row][0]
            to = ka // k_parts * n_v
            moved = pltpu.roll(part[0:1], (to - K_PER * n_bands) % 128, 1)
            line = line + jnp.where((lane >= to) & (lane < to + n_v), moved, 0.0)
        ph_out[row : row + 1, :] = line[:, : ph_out.shape[1]]


def finish(got, place, n_bands, n_v, k_parts, k_dev, n_modes):
    n_row, rows = got.shape[2:4]
    el, ph = pl.pallas_call(
        functools.partial(finish_kernel, n_bands, n_v, k_parts),
        in_specs=[pl.BlockSpec(memory_space=pltpu.SMEM), pl.BlockSpec(memory_space=pltpu.VMEM)],
        out_shape=[
            jax.ShapeDtypeStruct((n_bands, k_dev), F32),
            jax.ShapeDtypeStruct((n_row, n_modes), F32),
        ],
        scratch_shapes=[pltpu.VMEM((rows * K_PER, 128), F32)],
        compiler_params=VMEM,
        name="finish",
    )(place, pltpu.with_memory_space_constraint(got, pltpu.VMEM))
    return el.T, ph


def rotate_kernel(n_modes, n_bands, v_parts, coup_ref, rot_ref, out_ref):
    r = coup_ref.shape[1]
    pair = n_bands * n_bands
    rows = n_modes * r
    x = coup_ref[0].astype(F32)
    x = jnp.concatenate([x[:, c * pair : (c + 1) * pair] for c in range(n_modes)], axis=0).astype(BF16)
    rot = rot_ref[...].astype(F32)
    rot = jnp.sum(jnp.where(iota(rot.shape, 1) == pl.program_id(0), rot, 0.0), axis=1).astype(BF16)
    spread_v = (iota((rows, n_modes), 0) // r == iota((rows, n_modes), 1)).astype(BF16)
    spread_c = (iota((n_modes, rows), 1) // r == iota((n_modes, rows), 0)).astype(BF16)
    half = lax.dot_general(spread_v, rot, (((1,), (1,)), ((), ())), preferred_element_type=F32)
    full = jnp.dot(half.astype(BF16), spread_c, preferred_element_type=F32)
    same = iota((rows, rows), 0) % r == iota((rows, rows), 1) % r
    big = jnp.where(same, full, 0.0).astype(BF16)
    y = jnp.dot(big, x, preferred_element_type=F32)
    n_v = n_modes // v_parts
    wide = out_ref.shape[3]
    sent = n_bands // I_ROWS * n_v * n_bands
    for part in range(v_parts):
        pieces = []
        for i in range(I_ROWS):
            block = [
                y[v * r : (v + 1) * r, x * n_bands : (x + 1) * n_bands]
                for x in range(i, n_bands, I_ROWS)
                for v in range(part * n_v, (part + 1) * n_v)
            ]
            if wide > sent:
                block.append(jnp.zeros((r, wide - sent), F32))
            pieces.append(jnp.concatenate(block, axis=1))
        out_ref[part, 0] = jnp.concatenate(pieces, axis=0).astype(BF16)


def rotate(coupling, rotation, n_bands, v_parts):
    q, r, width = coupling.shape
    n_modes = rotation.shape[1]
    rows = I_ROWS * r
    cols = -(-(n_bands // I_ROWS * (n_modes // v_parts) * n_bands) // 128) * 128
    return pl.pallas_call(
        functools.partial(rotate_kernel, n_modes, n_bands, v_parts),
        grid=(q,),
        in_specs=[
            pl.BlockSpec((1, r, width), lambda a: (a, 0, 0)),
            pl.BlockSpec((n_modes, q, n_modes), lambda a: (0, 0, 0)),
        ],
        out_specs=pl.BlockSpec((v_parts, 1, rows, cols), lambda a: (0, a, 0, 0)),
        out_shape=jax.ShapeDtypeStruct((v_parts, q, rows, cols), BF16),
        compiler_params=VMEM,
        name="rotate_modes",
    )(
        pltpu.with_memory_space_constraint(coupling, pltpu.HBM),
        pltpu.with_memory_space_constraint(rotation.transpose(1, 0, 2), pltpu.HBM),
    )


def steps_of(k_loc):
    tiles = k_loc // (2 * K_PER)
    return tiles, -(-(tiles + 1) // UNROLL)


def prepare_kernel(
    n_bands, n_v, k_loc,
    freq_ref, start_ref, kq_ref, points_ref,
    wt_out, bd_out, gauss_out, occ_out,
    eig_scr, en_scr, keep_scr,
):
    g = pl.program_id(0)
    used = K_PER * n_bands
    k_all = points_ref.shape[0]
    at_en = points_ref.shape[1] - 128
    slots = 2 * K_PER
    scale = 1.0 / (SIGMA * math.sqrt(2.0))
    lane = iota((1, 128), 1)
    roll = lambda x, shift: pltpu.roll(x, shift % 128, 1) if shift % 128 else x

    @pl.when(g == 0)
    def _():
        en = roll(points_ref[:, at_en:].astype(F32), -(n_bands * n_bands % 128))
        lim = en[:, 2 * n_bands : 2 * n_bands + 1]
        en_scr[...] = jnp.where(lane < n_bands, en + roll(en, -n_bands), 0.0)
        keep = lane.astype(F32) < jnp.minimum(lim, float(n_bands))
        for i in range(n_bands):
            lo = i * n_bands
            tile = lo // 128 * 128
            block = roll(points_ref[:, tile : tile + 128].astype(F32), tile - lo)
            if lo + n_bands > tile + 128:
                more = roll(points_ref[:, tile + 128 : tile + 256].astype(F32), tile - lo)
                block = jnp.where(lane < tile + 128 - lo, block, more)
            eig_scr[pl.ds(i, k_all, stride=n_bands), :] = jnp.where(keep, block, 0.0)
        shape = (slots * n_bands, slots * n_bands)
        keep_scr[...] = (iota(shape, 0) // n_bands == iota(shape, 1) % slots).astype(BF16)

    by_band = (iota((n_bands, slots * n_bands), 0) == iota((n_bands, slots * n_bands), 1) // slots).astype(BF16)
    for step in range(PREPARED):
        t = g * PREPARED + step
        first = jnp.minimum(t * slots, k_loc - slots)
        v_tiles = []
        blocks = []
        for kg in range(2):
            vl = None
            level = None
            diagonal = []
            far_rows = []
            for x in range(K_PER):
                k = first + kg * K_PER + x
                near = k + start_ref[0]
                far = kq_ref[0, k]
                v = roll(eig_scr[pl.ds(pl.multiple_of(far * n_bands, 8), n_bands), :], n_bands * x)
                u = roll(eig_scr[pl.ds(pl.multiple_of(near * n_bands, 8), n_bands), :], n_bands * x)
                e = roll(en_scr[pl.ds(near, 1), :], n_bands * x)
                vl = v if vl is None else vl + v
                level = e if level is None else level + e
                diagonal.append(u)
                far_rows.append(jnp.broadcast_to(en_scr[pl.ds(far, 1), :], (n_bands, 128)))
            v_tiles.append(vl)
            blocks.append(jnp.concatenate(diagonal + [jnp.zeros((128 - used, 128), F32)], axis=0))
            cols = slice(kg * 128, (kg + 1) * 128)
            far_e = jnp.concatenate(far_rows + [jnp.zeros((128 - used, 128), F32)], axis=0).T[:n_bands]
            occ_out[step, :, cols] = jax.nn.sigmoid(-level / THERMAL_ENERGY_KT) - jax.nn.sigmoid(
                -far_e / THERMAL_ENERGY_KT
            )
            base = (far_e - level) * scale
            for v in range(0, n_v, 2):
                both = []
                for x in range(v, min(v + 2, n_v)):
                    d = base - freq_ref[0, x] * scale
                    both.append(jnp.exp(-(d * d)))
                rows = slice(v * n_bands, (v + len(both)) * n_bands)
                gauss_out[step, rows, cols] = jnp.concatenate(both, axis=0).astype(BF16)
        for kg in range(2):
            bd_out[step, kg] = blocks[kg].astype(BF16)
            turned = jnp.concatenate([blocks[kg][120:], blocks[kg][:120]], axis=0)
            bd_out[step, 2 + kg] = turned.astype(BF16)
        vl = jnp.concatenate(v_tiles, axis=1).astype(BF16)
        wt = lax.dot_general(vl, by_band, (((0,), (0,)), ((), ())), preferred_element_type=F32)
        wt = jnp.concatenate([wt[:used], wt[128 : 128 + used]], axis=0)
        wt_out[step] = wt.astype(BF16) * keep_scr[...]


def prepare(freq, start, kq, points, n_bands, n_v):
    k_loc = kq.shape[1]
    tiles, steps = steps_of(k_loc)
    tiles = max(tiles, steps * UNROLL)
    steps = -(-tiles // PREPARED)
    tiles = steps * PREPARED
    k_all = points.shape[0]
    wide = 2 * K_PER * n_bands
    smem = pl.BlockSpec(memory_space=pltpu.SMEM)
    shapes = ((wide, wide), (4, 128, 128), (n_v * n_bands, 256), (n_bands, 256))
    types = (BF16, BF16, BF16, F32)
    return pl.pallas_call(
        functools.partial(prepare_kernel, n_bands, n_v, k_loc),
        grid=(steps,),
        in_specs=[smem, smem, smem, pl.BlockSpec(memory_space=pltpu.VMEM)],
        out_specs=[
            pl.BlockSpec((PREPARED,) + x, lambda g, n=len(x): (g,) + (0,) * n) for x in shapes
        ],
        out_shape=[pltpu.HBM((tiles,) + x, t) for x, t in zip(shapes, types)],
        scratch_shapes=[
            pltpu.VMEM((k_all * n_bands, 128), F32),
            pltpu.VMEM((k_all, 128), F32),
            pltpu.VMEM((wide, wide), BF16),
        ],
        compiler_params=VMEM,
        name="prepare",
    )(freq, start, kq, points)


def swap_blocks(t_ref, n_bands, n_v):
    v_per = 128 // n_bands
    lane = iota((8, 128), 1)
    low = [n_bands * d % 128 for d in range(v_per + K_PER - 1)]
    from_low = [lane >= x for x in low]
    halves = [[[] for _ in range(v_per)] for _ in range(2)]
    for kg in range(2):
        for first in range(0, n_v, v_per):
            vg = first // v_per
            rolled = []
            for k in range(K_PER):
                row = (kg * K_PER + k) * n_bands
                block = t_ref[row : row + n_bands, vg * 128 : (vg + 1) * 128]
                rolled.append(pltpu.roll(block, n_bands * k, 1) if k else block)
            for x in range(min(v_per, n_v - first)):
                order = sorted(range(K_PER), key=lambda k: low[x + k])
                if low[x + order[-1]] + n_bands > 128:
                    order.insert(0, order[-1])
                for z in range(0, n_bands, 8):
                    mix = rolled[order[0]][z : z + 8]
                    for k in order[1:]:
                        mix = jnp.where(from_low[x + k], rolled[k][z : z + 8], mix)
                    halves[kg][x].append(mix)
    return [
        jnp.concatenate([jnp.concatenate(h[x], axis=0).astype(BF16) for h in halves], axis=1)
        for x in range(min(v_per, n_v))
    ]


def turned_blocks(bd_ref, x, n_bands):
    shift = n_bands * x % 128
    which = shift % 16 // 8
    shift -= 8 * which
    halves = []
    for kg in range(2):
        if shift:
            halves.append(
                jnp.concatenate(
                    [bd_ref[0, 2 * which + kg, 128 - shift :, :], bd_ref[0, 2 * which + kg, : 128 - shift, :]],
                    axis=0,
                )
            )
        else:
            halves.append(bd_ref[0, 2 * which + kg])
    zero = jnp.zeros((128, 128), BF16)
    return jnp.concatenate(
        [jnp.concatenate([halves[0], zero], axis=1), jnp.concatenate([zero, halves[1]], axis=1)], axis=0
    )


def tile_step(wt_ref, b_ref, t_new, t_old, bd_ref, gauss_ref, occ_ref, ph_scr, scale, n_bands, n_v):
    t_new[...] = jnp.dot(wt_ref[0], b_ref[0], preferred_element_type=F32)
    v_per = 128 // n_bands
    coupled = [
        jnp.dot(left, turned_blocks(bd_ref, x, n_bands), preferred_element_type=F32)
        for x, left in enumerate(swap_blocks(t_old, n_bands, n_v))
    ]
    occ = occ_ref[0]
    el = None
    for v in range(0, n_v, 2):
        count = min(2, n_v - v)
        gauss = gauss_ref[0, v * n_bands : (v + count) * n_bands, :].astype(F32)
        for x in range(count):
            at = (v + x) // v_per * n_bands
            c = coupled[(v + x) % v_per][at : at + n_bands]
            strength = c * c * gauss[x * n_bands : (x + 1) * n_bands]
            el = strength if el is None else el + strength
            weighed = strength * occ
            weighed = sum(weighed[z : z + 8] for z in range(0, n_bands, 8))
            weighed = weighed[:, :128] + weighed[:, 128:]
            ph_scr[v + x] += weighed if scale is None else weighed * scale
    el = jnp.sum(el, axis=0, keepdims=True)
    return [el[:, :128], el[:, 128:]]


def linewidth_kernel(n_bands, n_v, r, tiles, k_dev, el_scale, ph_scale, a_ref, phase_ref, *refs):
    refs = list(refs)
    take = lambda n: [refs.pop(0) for _ in range(n)]
    unroll = UNROLL
    sources = take(4)
    (send_out,) = take(1)
    held, (sems,) = take(4), take(1)
    wt_ref, bd_ref, gauss_ref, occ_ref = held
    (a_scr, b_scr, ph_scr, el_scr), t_scr = take(4), take(unroll)
    g = pl.program_id(0)
    last = pl.num_programs(0) - 1
    steps = -(-(tiles + 1) // unroll)
    n_src = a_ref.shape[0]
    v_per = 128 // n_bands
    cols = n_v * n_bands
    slots = 2 * K_PER

    def copy(which, step):
        part = pl.ds(step * unroll, unroll)
        return pltpu.make_async_copy(sources[which].at[part], held[which].at[part], sems.at[which, step])

    @pl.when(g == 0)
    def _():
        for which in range(4):
            copy(which, 0).start()
        lane = iota((1, 128), 1)
        for s in range(0, n_src, 2):
            for h in range(n_bands // I_ROWS):
                for vg in range(-(-n_v // v_per)):
                    lo = h * cols + vg * v_per * n_bands
                    tile, off = lo // 128 * 128, lo % 128
                    both = []
                    for x in (s, s + 1):
                        block = a_ref[x, :, tile : tile + 128].astype(F32)
                        if off:
                            block = pltpu.roll(block, 128 - off, 1)
                            if tile + 128 < a_ref.shape[2]:
                                more = a_ref[x, :, tile + 128 : tile + 256].astype(F32)
                                block = jnp.where(lane < 128 - off, block, pltpu.roll(more, 128 - off, 1))
                        both.append(block)
                    for i in range(I_ROWS):
                        here = slice(i * r, (i + 1) * r)
                        a_scr[h * I_ROWS + i, s * r : (s + 2) * r, vg * 128 : (vg + 1) * 128] = (
                            jnp.concatenate([both[0][here], both[1][here]], axis=0).astype(BF16)
                        )
        for i in range(0, n_bands, 2):
            b0 = jnp.dot(phase_ref[...], a_scr[i], preferred_element_type=F32)
            b1 = jnp.dot(phase_ref[...], a_scr[i + 1], preferred_element_type=F32)
            for t in range(tiles):
                here = slice(t * slots, (t + 1) * slots)
                b_scr[t, i * slots : (i + 2) * slots, :] = jnp.concatenate(
                    [b0[here], b1[here]], axis=0
                ).astype(BF16)
        t_scr[-1][...] = jnp.zeros_like(t_scr[-1])
        ph_scr[...] = jnp.zeros_like(ph_scr)

    for which in range(4):
        copy(which, g).wait()

    @pl.when(g < last)
    def _():
        for which in range(4):
            copy(which, g + 1).start()

    def tile_of(ref, n):
        return ref.at[pl.ds(jnp.clip(unroll * g + n, 0, tiles - 1), 1)]

    el = []
    for x in range(unroll):
        beyond = (steps - 1) * unroll + x - 1 >= tiles
        scale = jnp.where(g < last, 1.0, 0.0) if beyond else None
        el += tile_step(
            tile_of(wt_ref, x), tile_of(b_scr, x), t_scr[x], t_scr[x - 1], tile_of(bd_ref, x - 1),
            tile_of(gauss_ref, x - 1), tile_of(occ_ref, x - 1), ph_scr, scale, n_bands, n_v,
        )
    stride = el_scr.shape[0] // steps
    el_scr[pl.ds(g * stride, 2 * unroll), :] = jnp.concatenate(el, axis=0)

    @pl.when(g == last)
    def _():
        used = K_PER * n_bands
        n_ka, n_pb, n_row, n_rows, _ = send_out.shape
        sums = jnp.sum(ph_scr[...], axis=1)
        sums = jnp.concatenate([sums, jnp.zeros((128 - n_v, 128), F32)], axis=0).T
        sums = pltpu.roll(jnp.sum(sums, axis=0, keepdims=True) * ph_scale, used, 1)
        groups = [el_scr[x * stride : x * stride + 2 * unroll, :] for x in range(steps)]
        groups = jnp.concatenate(groups, axis=0) * el_scale
        lane = iota((n_rows, 128), 1)
        for d in range(n_ka * n_row):
            lo = 2 + d * n_rows
            part = jnp.where(lane < used, groups[lo : lo + n_rows], sums)
            for pb in range(n_pb):
                send_out[d // n_row, pb, d % n_row] = part


def linewidths(a, phase, prepared, k_loc, k_dev, n_row, n_pb, n_bands, n_v, r, el_scale, ph_scale):
    wt, bd, gauss, occ = prepared
    tiles, steps = steps_of(k_loc)
    lanes = -(-n_v // (128 // n_bands)) * 128
    wide = 2 * K_PER * n_bands
    depth = a.shape[0] * r
    a = pltpu.with_memory_space_constraint(a, pltpu.VMEM)
    tables = [pltpu.with_memory_space_constraint(x, pltpu.HBM) for x in (wt, bd, gauss, occ)]
    n_rows = k_dev // K_PER
    n_ka = k_loc // k_dev // n_row
    return pl.pallas_call(
        functools.partial(linewidth_kernel, n_bands, n_v, r, tiles, k_dev, el_scale, ph_scale),
        grid=(steps,),
        in_specs=[pl.BlockSpec(memory_space=pltpu.VMEM)] * 2
        + [pl.BlockSpec(memory_space=pltpu.HBM)] * len(tables),
        out_specs=pl.BlockSpec((n_ka, n_pb, n_row, n_rows, 128), lambda g: (0,) * 5),
        out_shape=jax.ShapeDtypeStruct((n_ka, n_pb, n_row, n_rows, 128), F32),
        scratch_shapes=[pltpu.VMEM(x.shape, x.dtype) for x in tables]
        + [pltpu.SemaphoreType.DMA((len(tables), steps))]
        + [
            pltpu.VMEM((n_bands, depth, lanes), BF16),
            pltpu.VMEM((tiles, wide, lanes), BF16),
            pltpu.VMEM((n_v, 8, 128), F32),
            pltpu.VMEM((steps * -(-2 * UNROLL // 8) * 8, 128), F32),
        ]
        + [pltpu.VMEM((wide, lanes), F32)] * UNROLL,
        compiler_params=VMEM,
        name="linewidths",
    )(a, phase, *tables)


def on_device(coupling, rotation, freq, eigvec, energies, window, kq_index, kpoints, lattice):
    plane = ("ka", "row")
    everywhere = ("ka", "pb", "row")
    n_ka = lax.axis_size("ka")
    n_row = lax.axis_size("row")
    n_pb = lax.axis_size("pb")
    n_group = n_ka * n_row
    k_dev, n_bands = eigvec.shape[:2]
    q_dev, n_modes = rotation.shape[:2]
    assert q_dev == n_row
    pair = n_bands * n_bands
    total_k = k_dev * n_group
    total_q = q_dev * n_pb
    v_parts = math.gcd(n_modes, n_ka)
    k_parts = n_ka // v_parts
    n_v = n_modes // v_parts
    k_loc = total_k // k_parts
    ka_pos = lax.axis_index("ka")
    row_pos = lax.axis_index("row")
    pb_pos = lax.axis_index("pb")

    points = pack(eigvec, energies, window, n_group)
    mine = lax.all_to_all(points, plane, 0, 0, tiled=True)
    other = lax.ppermute(mine, "row", [(i, i ^ 1) for i in range(n_row)])
    odd = row_pos % 2 == 1
    points = jnp.concatenate([jnp.where(odd, other, mine), jnp.where(odd, mine, other)], axis=1)
    points = points.reshape(total_k, -1)

    pad = -coupling.shape[1] % 8
    if pad:
        coupling = jnp.pad(coupling, ((0, 0), (0, pad), (0, 0)))
    r = coupling.shape[1]
    rotated = rotate(coupling, rotation, n_bands, v_parts)
    if k_parts > 1:
        rotated = jnp.repeat(rotated, k_parts, axis=0)
    rotated = rotated.reshape((n_group,) + rotated.shape[2:])
    a = lax.all_to_all(rotated, plane, 0, 0, tiled=True)
    k_start = (ka_pos % k_parts) * k_loc
    kp = lax.dynamic_slice_in_dim(kpoints, k_start, k_loc, 0)
    phase = phase_rows(lattice, kp)
    if pad:
        phase = jnp.pad(phase.reshape(k_loc, n_group, r - pad), ((0, 0), (0, 0), (0, pad)))
        phase = phase.reshape(k_loc, n_group * r)
    kq = lax.dynamic_slice(kq_index, (row_pos, k_start), (1, k_loc))
    v_start = (ka_pos // k_parts) * n_v
    freq_mine = lax.dynamic_slice(freq, (row_pos, v_start), (1, n_v))
    points = pltpu.with_memory_space_constraint(points, pltpu.VMEM)
    prepared = prepare(freq_mine, k_start[None], kq, points, n_bands, n_v)
    norm = 1.0 / (math.sqrt(2.0 * math.pi) * SIGMA)
    send = linewidths(
        a, phase, prepared, k_loc, k_dev, n_row, n_pb, n_bands, n_v, r,
        norm / (total_q * n_modes * n_bands), norm / (total_k * n_bands),
    )
    if k_parts > 1:
        used = K_PER * n_bands
        rest = jnp.where(jnp.arange(128) < used, 0.0, send[:1])
        rest = jnp.broadcast_to(rest, (n_ka,) + send.shape[1:])
        send = lax.dynamic_update_slice_in_dim(rest, send, k_start // (k_dev * n_row), 0)
    got = lax.all_to_all(
        send.reshape((n_group * n_pb,) + send.shape[3:]), everywhere, 0, 0, tiled=True
    ).reshape(send.shape)
    place = pb_pos[None].astype(jnp.int32)
    electron, phonon = finish(got, place, n_bands, n_v, k_parts, k_dev, n_modes)
    return (electron, phonon)


def solution(mesh):
    return jax.shard_map(
        on_device,
        mesh=mesh,
        in_specs=(
            P("pb", ("ka", "row"), None),
            P("pb", None, None),
            P("pb", None),
            P(("ka", "row"), None, None),
            P(("ka", "row"), None),
            P(("ka", "row")),
            P("pb", None),
            P(),
            P(),
        ),
        out_specs=(P(("ka", "row"), None), P("pb", None)),
        check_vma=False,
    )
```
